256 devices in a mesh: grp: 32 (over x, y, core), tp: 8 (over z).
Axes of the slice: x: 4, y: 4, z: 8, core: 2. Of those that a mesh axis runs over, the one named last changes fastest.
Arguments:
- queries: bfloat16 [32, 128, 8192], P('grp', None, 'tp'), may hold values from -10.5 to 10.5
- span_kv: bfloat16 [32, 128, 8, 256], P('grp', None, 'tp'), may hold values from -6 to 6
- cache: bfloat16 [1536, 128, 8, 256], P('grp', None, 'tp'), may hold values from -6 to 6
- block_owner: int32 [1536, 1], P('grp'), may hold values from 0 to 31; in each aligned block of 48 rows (0 to 47, 48 to 95, ...) at most 2 rows name the same one
- block_fill: int32 [1536, 1], P('grp'), may hold values from 1 to 128
- out_weight: bfloat16 [8192, 8192], P('tp', 'grp'), may hold values from -0.25 to 0.25
Outputs:
- attn_out: bfloat16 [4096, 8192], P('tp', 'grp')
The draws below stay inside these ranges and needn't reach their ends.
Inputs may be any that keep to these rules, and one draw needn't show every extreme that they name: `block_owner`: among the 48 blocks stored on one group (rows g * 48 to g * 48 + 47) no response is named more than 2 times; every response owns at least one block.
All inputs are finite; a program needn't handle non-finite values.
Results may differ from the reference program's by a relative error of at most 0.022.
Values may be sent and summed in bfloat16 or wider, within the bound.
A program may use at most 128 MiB of HBM per device.

```python
import math
import jax
import jax.numpy as jnp
import numpy as np
from jax import lax

D = 8192
HEADS = 64
KVH = 8
HD = 128
C = 128
KB = 128
CAP = 2
SLOTS = 48
RESP = 32
N_GRP = 32


def draw_queries(key, part):
    key = jax.random.fold_in(key, 11)
    shape = (RESP, C, HEADS * HD)
    base = jnp.clip(2.5 * jax.random.normal(key, shape, jnp.float32), -10.5, 10.5)
    return base.astype(jnp.bfloat16)


def draw_cache(key, part):
    key = jax.random.fold_in(key, 23)
    first = jax.random.fold_in(key, 0)
    shape = (N_GRP * SLOTS, KB, KVH, 2 * HD)
    base = jnp.clip(jax.random.normal(first, shape, jnp.float32), -6.0, 6.0)
    return base.astype(jnp.bfloat16)


def plant(values, key, smallest, top_value):
    spot = [jax.random.randint(jax.random.fold_in(key, axis), (), 0, length) for axis, length in enumerate(values.shape)]
    widest = values.shape.index(max(values.shape))
    beside = spot[:widest] + [(spot[widest] + 1) % values.shape[widest]] + spot[widest + 1:]
    return values.at[tuple(spot)].set(smallest).at[tuple(beside)].set(top_value)


def steps_of(rng, extent, cuts, smallest, largest):
    def one(axis_at, blocks):
        steps = jax.random.uniform(jax.random.fold_in(jax.random.fold_in(rng, 6), axis_at), (blocks,), jnp.float32, smallest / len(cuts), largest / len(cuts))
        return jnp.repeat(jnp.exp(steps), extent[axis_at] // blocks).reshape((-1,) + (1,) * (len(extent) - axis_at - 1))

    factor_of = one(*cuts[0])
    for cut in cuts[1:]:
        factor_of = factor_of * one(*cut)
    return factor_of


def assign_block(key, own, number, rows, amount, top, most, skew):
    ranking = jax.random.permutation(key, amount)
    packed, usual = shares(amount, rows * top, most, skew, True), shares(amount, rows * top, most, skew, False)
    places = jnp.arange(amount)

    def named(lengths, turn):
        used = int((lengths > 0).sum())
        fixed = max(1, used // 4)
        shifted = fixed + (places - fixed + turn * (used - fixed)) % max(1, amount - fixed)
        return jnp.zeros((amount,), jnp.int32).at[ranking[jnp.where(places < fixed, places, shifted)]].set(jnp.asarray(lengths, jnp.int32))

    lengths = jnp.where(number % 4 == 0, named(packed, number // 4), named(usual, number - number // 4 - 1))
    mixed = jax.random.permutation(jax.random.fold_in(own, 3), amount)
    source_of, taker = mixed[0:amount // 2 * 2:2], mixed[1:amount // 2 * 2:2]
    slack = jnp.minimum(lengths[source_of] - 1, most - lengths[taker]) // 2
    slack = jnp.where((source_of == ranking[0]) | (taker == ranking[0]) | (lengths[taker] == 0), 0, jnp.maximum(slack, 0))
    shifted = jax.random.randint(jax.random.fold_in(own, 4), (amount // 2,), 0, 1 << 20) % (slack + 1)
    lengths = lengths.at[source_of].add(-shifted).at[taker].add(shifted)
    members = jnp.searchsorted(jnp.cumsum(lengths), jnp.arange(rows * top), side="right").astype(jnp.int32)
    grid = members.reshape(top, rows).T
    grid = grid[jax.random.permutation(jax.random.fold_in(own, 1), rows)]
    turn = jax.random.randint(jax.random.fold_in(own, 2), (rows, 1), 0, top)
    return jnp.take_along_axis(grid, (jnp.arange(top)[None, :] + turn) % top, axis=1)


def shares(amount, total, bound, lean, full):
    weights = [(1 << 20) // math.isqrt(standing ** lean) + 1 for standing in range(1, amount + 1)]
    largest = bound if full else min(bound, max(-(-total // amount), total * weights[0] // sum(weights)))
    least = 1 if total - largest >= amount - 1 else 0
    holding, spare = [largest] + [least] * (amount - 1), total - largest - least * (amount - 1)
    while spare > 0:
        candidates = [i for i in range(1, amount) if holding[i] < largest] or [i for i in range(1, amount) if holding[i] < bound]
        mass, remaining = sum([weights[i] for i in candidates]), spare
        for i in candidates:
            addition = min(bound - holding[i], max(1, remaining * weights[i] // mass), spare)
            holding[i] = holding[i] + addition
            spare = spare - addition
    return np.array(holding)


def noise(rng, shape, scale, bound, cuts=(), held_as=jnp.bfloat16):
    factor_of = steps_of(rng, shape, cuts, -0.22, 0.18) if cuts else 1.0
    values = jax.random.normal(rng, shape, jnp.float32) * scale * factor_of
    return jnp.minimum(jnp.maximum(values, -bound), bound).astype(held_as)


def setup_inputs(seed: int = 0) -> dict:
    arg_keys = jax.random.split(jax.random.key(seed), 7)
    queries = draw_queries(jax.random.fold_in(arg_keys[6], 71), 0)
    span_kv = noise(arg_keys[1], (RESP, C, KVH, 2 * HD), 1.0, 6.0, ((0, 32), (2, 8)))
    cache = draw_cache(jax.random.fold_in(arg_keys[6], 71), 0)
    block_owner_keys = jax.random.split(jax.random.fold_in(arg_keys[3], 1), (N_GRP * SLOTS) // SLOTS)
    block_owner_turns = jax.random.permutation(jax.random.fold_in(arg_keys[3], 3), (N_GRP * SLOTS) // SLOTS)
    block_owner = jax.vmap(lambda own, number: assign_block(jax.random.fold_in(arg_keys[3], 2), own, number, SLOTS, N_GRP, 1, CAP, 2))(block_owner_keys, block_owner_turns).reshape((N_GRP * SLOTS, 1))
    block_fill = plant(jax.random.randint(arg_keys[4], (N_GRP * SLOTS, 1), 1, KB + 1), jax.random.fold_in(arg_keys[4], 1), 1, KB).astype(jnp.int32)
    out_weight = noise(arg_keys[5], (HEADS * HD, D), (HEADS * HD // 16) ** -0.5, 0.25, ((0, 8), (1, 32)))
    return dict(queries=queries, span_kv=span_kv, cache=cache, block_owner=block_owner, block_fill=block_fill, out_weight=out_weight)


def reference(queries, span_kv, cache, block_owner, block_fill, out_weight):
    owners = block_owner[:, 0].astype(jnp.int32)
    fills = block_fill[:, 0].astype(jnp.int32)
    resp = queries.shape[0]
    width = N_GRP * CAP
    counts = jnp.sum((owners[:, None] == jnp.arange(resp, dtype=jnp.int32)[None, :]).astype(jnp.int32), 0).astype(jnp.int32)
    starts = (jnp.cumsum(counts) - counts).astype(jnp.int32)
    order = jnp.argsort(owners, stable=True).astype(jnp.int32)
    padded = jnp.concatenate([order, jnp.zeros((width,), jnp.int32)])
    group = HEADS // KVH
    scale = 1.0 / (HD ** 0.5)
    causal = jnp.arange(C)[None, :] <= jnp.arange(C)[:, None]

    def one(r):
        index = lax.dynamic_slice(padded, (starts[r].astype(jnp.int32),), (width,))
        blocks = cache[index].reshape(width * KB, KVH, 2 * HD)
        valid = jnp.arange(width, dtype=jnp.int32) < counts[r]
        inside = jnp.arange(KB, dtype=jnp.int32)[None, :] < fills[index][:, None]
        seen = (valid[:, None] & inside).reshape(width * KB)
        mask = jnp.concatenate([jnp.broadcast_to(seen[None, :], (C, width * KB)), causal], 1)
        every = jnp.concatenate([blocks, span_kv[r]], 0).astype(jnp.float32)
        query = queries[r].reshape(C, KVH, group, HD).astype(jnp.float32)
        scores = jnp.einsum('cjgd,njd->jgcn', query, every[:, :, :HD]) * scale
        scores = jnp.where(mask[None, None], scores, -1e30)
        top = jnp.max(scores, -1, keepdims=True)
        expo = jnp.exp(scores - top)
        weights = (expo / jnp.sum(expo, -1, keepdims=True)).astype(jnp.bfloat16)
        heads = jnp.einsum('jgcn,njd->cjgd', weights.astype(jnp.float32), every[:, :, HD:])
        return heads.astype(jnp.bfloat16).reshape(C, HEADS * HD)

    heads_out = lax.map(one, jnp.arange(resp, dtype=jnp.int32))
    flat = heads_out.reshape(resp * C, HEADS * HD)
    return jnp.dot(flat, out_weight, preferred_element_type=jnp.float32).astype(jnp.bfloat16)
```

```python
import functools

import jax
import jax.numpy as jnp
from jax import lax
from jax.experimental import pallas as pl
from jax.experimental.pallas import tpu as pltpu
from jax.sharding import PartitionSpec as P

MESH = pl.DeviceIdType.MESH
NX, NY, NC, NZ = 4, 4, 2, 8
GRP = NX * NY * NC
CAP = 2
KB = 128
HD = 128
NEW = 128
WIDTH = 1024
FEAT = 256
CHUNK = NEW // NZ
NEG = -1e30
LOG2E = 1.4426950408889634
F32 = jnp.float32
BF16 = jnp.bfloat16
ORDER = ((0, 0), (3, 0), (1, 0), (0, 3), (0, 1), (2, 0), (3, 3), (3, 1), (1, 3), (1, 1), (0, 2), (2, 3), (2, 1), (3, 2), (1, 2), (2, 2))


def table_kernel(owner_ref, fill_ref, table_ref, count_ref):
    slots = owner_ref.shape[0]

    def clear(i, c):
        count_ref[i] = 0
        table_ref[2 * i] = 0
        table_ref[2 * i + 1] = 0
        table_ref[2 * GRP + i] = 0
        return c

    lax.fori_loop(0, GRP, clear, 0)

    def place(b, c):
        own = owner_ref[b]
        rank = count_ref[own]
        count_ref[own] = rank + 1
        table_ref[2 * own + rank] = b
        fill = fill_ref[b]
        held = table_ref[2 * GRP + own]
        table_ref[2 * GRP + own] = held + jnp.where(rank == 0, fill, fill * 256)
        return c

    lax.fori_loop(0, slots, place, 0)


def main_kernel(
    table, q_ref, span_ref, cache_ref, w_ref, o_ref,
    send, sfill, recv, rfill, qs, m, acc, wfull, heads, gath, total, zout, obuf,
    kv_s, kv_r, f_s, f_r, w_s, w_r, a_s, a_r, g_s, g_r, b_s, b_r, o_s, o_r,
):
    g = lax.axis_index("grp")
    t = lax.axis_index("tp")
    x, y, c = g // (NY * NC), (g // NC) % NY, g % NC

    def at(px, py, pc):
        return (px % NX) * (NY * NC) + (py % NY) * NC + pc

    sib = at(x, y, 1 - c)

    def copy(src, dst, ssem, rsem, dev):
        return pltpu.make_async_remote_copy(
            src_ref=src, dst_ref=dst, send_sem=ssem, recv_sem=rsem, device_id=dev, device_id_type=MESH
        )

    barrier = pltpu.get_barrier_semaphore()

    def greet(s, k):
        pl.semaphore_signal(barrier, inc=1, device_id=((g + s) % GRP, t), device_id_type=MESH)
        return k

    lax.fori_loop(1, GRP, greet, 0)
    for s in range(1, NZ):
        pl.semaphore_signal(barrier, inc=1, device_id=(g, (t + s) % NZ), device_id_type=MESH)
    pl.semaphore_wait(barrier, GRP - 1 + NZ - 1)

    up, down = (t + 1) % NZ, (t + NZ - 1) % NZ
    wfull[t] = w_ref[...]
    half = WIDTH // 2

    def wcopy(n, z, lo, size, k, dev):
        part = wfull.at[z, pl.ds(lo, size)]
        return copy(part, part, w_s.at[n], w_r.at[z, k], (g, dev))

    wsends = [wcopy(0, t, 0, WIDTH, 0, up), wcopy(1, t, 0, WIDTH, 0, down)]
    for d in wsends:
        d.start()

    def wpass(j, lo, hi):
        low, high = (t + NZ - j) % NZ, (t + j) % NZ
        wcopy(0, low, 0, WIDTH, 0, up).wait_recv()
        d0 = wcopy(2 * j, low, lo, hi, 0, up)
        d0.start()
        wcopy(0, high, 0, WIDTH, 0, down).wait_recv()
        d1 = wcopy(2 * j + 1, high, half if hi < WIDTH else 0, hi, 1 if hi < WIDTH else 0, down)
        d1.start()
        wsends.extend([d0, d1])

    def where_to(s):
        o = (s * 11) % GRP
        return o // (NY * NC), (o // NC) % NY, o % NC

    def load(dst):
        first = cache_ref[table[2 * dst]]
        second = cache_ref[table[2 * dst + 1]]
        fills = jnp.full((1, KB), table[2 * GRP + dst], jnp.int32)
        return first, second, fills

    def kv_copy(dst, s):
        return copy(send.at[dst], recv.at[g], kv_s.at[s], kv_r.at[g], (dst, t))

    def fill_copy(dst, s):
        return copy(sfill.at[dst], rfill.at[g], f_s.at[s], f_r.at[g], (dst, t))

    def give(s, k):
        dx, dy, dc = where_to(s)
        dst = at(x + dx, y + dy, (c + dc) % NC)
        first, second, fills = load(dst)
        send[dst, :KB] = first
        send[dst, KB:] = second
        sfill[dst] = fills
        kv_copy(dst, s).start()
        fill_copy(dst, s).start()
        return k

    lax.fori_loop(1, GRP, give, 0)
    first, second, fills = load(g)
    recv[g, :KB] = first
    recv[g, KB:] = second
    rfill[g] = fills

    heads_n = WIDTH // HD
    for h in range(heads_n):
        qs[h * NEW:(h + 1) * NEW, :] = q_ref[:, h * HD:(h + 1) * HD]
    factor = LOG2E / HD**0.5
    blk = 256
    ones = jnp.ones((CAP * KB, HD), BF16)

    def scores(rows, keys):
        return lax.dot_general(qs[rows, :], keys, (((1,), (1,)), ((), ())), preferred_element_type=F32) * factor

    span_k, span_v = span_ref[:, :HD], span_ref[:, HD:]
    span_aug = jnp.concatenate([span_v, ones[:NEW]], 1)
    row = lax.broadcasted_iota(jnp.int32, (blk, NEW), 0) % NEW
    col = lax.broadcasted_iota(jnp.int32, (blk, NEW), 1)
    for qb in range(WIDTH // blk):
        rows = pl.ds(qb * blk, blk)
        s = jnp.where(col <= row, scores(rows, span_k), NEG)
        top = jnp.max(s, 1, keepdims=True)
        m[rows, :] = jnp.broadcast_to(top, (blk, HD))
        p = jnp.exp2(s - top).astype(BF16)
        acc[rows, :] = jnp.dot(p, span_aug, preferred_element_type=F32)

    lane = lax.broadcasted_iota(jnp.int32, (1, KB), 1)

    def attend(src):
        fills = rfill[src]
        bias = jnp.concatenate(
            [jnp.where(lane < fills % 256, 0.0, NEG), jnp.where(lane < fills // 256, 0.0, NEG)], 1
        )
        keys = recv[src, :, :HD]
        vals = jnp.concatenate([recv[src, :, HD:], ones], 1)
        for qb in range(WIDTH // blk):
            rows = pl.ds(qb * blk, blk)
            s = scores(rows, keys) + bias
            old = m[rows, :]
            new = jnp.maximum(old, jnp.max(s, 1, keepdims=True))
            alpha = jnp.exp2(old - new)
            p = jnp.exp2(s - jnp.concatenate([new, new], 1)).astype(BF16)
            part = jnp.dot(p, vals, preferred_element_type=F32)
            acc[rows, :] = acc[rows, :] * jnp.concatenate([alpha, alpha], 1) + part
            m[rows, :] = new

    attend(g)

    def take(s, k):
        dx, dy, dc = where_to(s)
        src = at(x + NX - dx, y + NY - dy, (c + dc) % NC)
        copy(send.at[src], recv.at[src], kv_s.at[s], kv_r.at[src], (src, t)).wait_recv()
        copy(sfill.at[src], rfill.at[src], f_s.at[s], f_r.at[src], (src, t)).wait_recv()
        attend(src)
        return k

    lax.fori_loop(1, 9, take, 0)
    wpass(1, 0, WIDTH)
    lax.fori_loop(9, 17, take, 0)
    wpass(2, 0, WIDTH)
    lax.fori_loop(17, 25, take, 0)
    wpass(3, 0, half)
    total[...] = jnp.zeros_like(total)
    lax.fori_loop(25, GRP, take, 0)

    for h in range(heads_n):
        rows = pl.ds(h * NEW, NEW)
        out = (acc[rows, :HD] / acc[rows, HD:]).astype(BF16)
        heads[:, :, h * HD:(h + 1) * HD] = out.reshape(NZ, CHUNK, HD)

    def spread(s, k):
        z = (t + s) % NZ
        copy(heads.at[z], gath.at[g, t], a_s.at[s], a_r.at[t], (g, z)).start()
        return k

    lax.fori_loop(1, NZ, spread, 0)
    gath[g, t] = heads[t]

    def spread_in(s, k):
        z = (t + s) % NZ
        copy(heads.at[z], gath.at[g, z], a_s.at[s], a_r.at[z], (g, z)).wait_recv()
        return k

    lax.fori_loop(1, NZ, spread_in, 0)

    sends = []

    def piece(owner, lo, size):
        return gath.at[owner, pl.ds(lo, size)]

    def push(owner, lo, size, quarter, dev):
        part = piece(owner, lo, size)
        d = copy(part, part, g_s.at[len(sends)], g_r.at[owner, quarter], (dev, t))
        d.start()
        sends.append(d)

    def arrived(owner, lo, size, quarter):
        part = piece(owner, lo, size)
        copy(part, part, g_s.at[0], g_r.at[owner, quarter], (sib, t)).wait_recv()

    def place(h, d1, d2, pc):
        return at(x + d1, y + d2, pc) if h == 0 else at(x + d2, y + d1, pc)

    def share(h, owner):
        part = piece(owner, 4 * h, 4)
        d = copy(part, part, b_s.at[len(shared)], b_r.at[owner, h], (sib, t))
        d.start()
        shared.append(d)

    shared = []

    def event(h, d1, d2):
        owner = place(h, d1, d2, c)
        lo = 4 * h
        q = 2 * h
        fwd1, back1 = place(h, 1, 0, c), place(h, 3, 0, c)
        fwd2, back2 = place(h, 0, 1, c), place(h, 0, 3, c)
        last = d2 if d2 else d1
        if last == 2:
            arrived(owner, lo, 2, q)
            arrived(owner, lo + 2, 2, q + 1)
        elif last:
            arrived(owner, lo, 4, q)
        if d2 == 0:
            if d1 == 0:
                push(owner, lo, 4, q, fwd1)
                push(owner, lo, 4, q, back1)
            elif d1 == 3:
                push(owner, lo, 2, q, fwd1)
            elif d1 == 1:
                push(owner, lo + 2, 2, q + 1, back1)
            push(owner, lo, 4, q, fwd2)
            push(owner, lo, 4, q, back2)
        elif d2 == 3:
            push(owner, lo, 2, q, fwd2)
        elif d2 == 1:
            push(owner, lo + 2, 2, q + 1, back2)
        share(h, owner)

    def multiply(h, d2):
        owners = [place(h, d1, d2, pc) for d1 in range(4) for pc in range(2)]
        for d1 in range(4):
            other = place(h, d1, d2, 1 - c)
            part = piece(other, 4 * h, 4)
            copy(part, part, b_s.at[0], b_r.at[other, h], (sib, t)).wait_recv()

        def step(k, sum_):
            z = 4 * h + k
            rows = jnp.concatenate([gath[o, z] for o in owners], 0)
            return sum_ + jnp.dot(rows, wfull[z], preferred_element_type=F32)

        got = lax.fori_loop(0, 4, step, jnp.zeros((len(owners) * CHUNK, FEAT), F32))
        for i, o in enumerate(owners):
            total[o] = total[o] + got[i * CHUNK:(i + 1) * CHUNK]

    for n, (d1, d2) in enumerate(ORDER):
        for h in range(2):
            event(h, d1, d2)
        if n == 0:
            opposite = (t + 4) % NZ
            wcopy(0, opposite, 0, half, 0, up).wait_recv()
            wcopy(0, opposite, half, half, 1, down).wait_recv()
        done = {6: 0, 12: 3, 13: 1, 15: 2}.get(n)
        if done is not None:
            for h in range(2):
                multiply(h, done)

    zout[...] = total[...].astype(BF16)
    per = GRP // NZ

    def ocopy(s):
        z = (t + s) % NZ
        return copy(zout.at[pl.ds(z * per, per)], obuf.at[:, t], o_s.at[s], o_r.at[t], (g, z))

    def hand(s, k):
        ocopy(s).start()
        return k

    lax.fori_loop(1, NZ, hand, 0)
    obuf[:, t] = zout[pl.ds(t * per, per)]

    def hand_in(s, k):
        z = (t + s) % NZ
        copy(zout.at[pl.ds(z * per, per)], obuf.at[:, z], o_s.at[s], o_r.at[z], (g, z)).wait_recv()
        return k

    lax.fori_loop(1, NZ, hand_in, 0)
    o_ref[...] = obuf[...]

    def sent(s, k):
        dx, dy, dc = where_to(s)
        dst = at(x + dx, y + dy, (c + dc) % NC)
        kv_copy(dst, s).wait_send()
        fill_copy(dst, s).wait_send()
        return k

    lax.fori_loop(1, GRP, sent, 0)

    def sent_z(s, k):
        z = (t + s) % NZ
        copy(heads.at[z], gath.at[g, t], a_s.at[s], a_r.at[t], (g, z)).wait_send()
        ocopy(s).wait_send()
        return k

    lax.fori_loop(1, NZ, sent_z, 0)
    for d in wsends + sends + shared:
        d.wait_send()


def body(queries, span_kv, cache, block_owner, block_fill, out_weight):
    slots = cache.shape[0]
    smem = pl.BlockSpec(memory_space=pltpu.SMEM)
    vmem = pl.BlockSpec(memory_space=pltpu.VMEM)
    table = pl.pallas_call(
        table_kernel,
        out_shape=jax.ShapeDtypeStruct((3 * GRP,), jnp.int32),
        in_specs=[smem, smem],
        out_specs=smem,
        scratch_shapes=[pltpu.SMEM((GRP,), jnp.int32)],
    )(block_owner.reshape(slots), block_fill.reshape(slots))
    dma = pltpu.SemaphoreType.DMA
    out = pl.pallas_call(
        main_kernel,
        out_shape=jax.ShapeDtypeStruct((GRP // NZ, NZ, CHUNK, FEAT), BF16),
        in_specs=[smem, vmem, vmem, vmem, vmem],
        out_specs=vmem,
        scratch_shapes=[
            pltpu.VMEM((GRP, CAP * KB, 2 * HD), BF16),
            pltpu.VMEM((GRP, 1, KB), jnp.int32),
            pltpu.VMEM((GRP, CAP * KB, 2 * HD), BF16),
            pltpu.VMEM((GRP, 1, KB), jnp.int32),
            pltpu.VMEM((WIDTH, HD), BF16),
            pltpu.VMEM((WIDTH, HD), F32),
            pltpu.VMEM((WIDTH, 2 * HD), F32),
            pltpu.VMEM((NZ, WIDTH, FEAT), BF16),
            pltpu.VMEM((NZ, CHUNK, WIDTH), BF16),
            pltpu.VMEM((GRP, NZ, CHUNK, WIDTH), BF16),
            pltpu.VMEM((GRP, CHUNK, FEAT), F32),
            pltpu.VMEM((GRP, CHUNK, FEAT), BF16),
            pltpu.VMEM((GRP // NZ, NZ, CHUNK, FEAT), BF16),
            dma((GRP,)), dma((GRP,)), dma((GRP,)), dma((GRP,)),
            dma((NZ,)), dma((NZ, 2)),
            dma((NZ,)), dma((NZ,)),
            dma((40,)), dma((GRP, 4)),
            dma((32,)), dma((GRP, 2)),
            dma((NZ,)), dma((NZ,)),
        ],
        compiler_params=pltpu.CompilerParams(
            collective_id=0, has_side_effects=True, vmem_limit_bytes=50 * 1024 * 1024
        ),
    )(
        table,
        queries.reshape(NEW, WIDTH),
        span_kv.reshape(NEW, 2 * HD),
        cache.reshape(slots, KB, 2 * HD),
        out_weight,
    )
    return out.reshape(GRP // NZ * NEW, FEAT)


def solution(mesh):
    in_specs = (
        P("grp", None, "tp"),
        P("grp", None, "tp", None),
        P("grp", None, "tp", None),
        P("grp", None),
        P("grp", None),
        P("tp", "grp"),
    )
    out_specs = P("tp", "grp")
    return jax.shard_map(body, mesh=mesh, in_specs=in_specs, out_specs=out_specs, check_vma=False)
```

```python
import functools

import jax
import jax.numpy as jnp
from jax import lax
from jax.experimental import pallas as pl
from jax.experimental.pallas import tpu as pltpu
from jax.sharding import PartitionSpec as P

MESH = pl.DeviceIdType.MESH
NX, NY, NC, NZ = 4, 4, 2, 8
GRP = NX * NY * NC
CAP = 2
KB = 128
HD = 128
NEW = 128
WIDTH = 1024
FEAT = 256
CHUNK = NEW // NZ
NEG = -1e30
AHEAD = 31
STOPS = (1, 9, 17)
VMEM_LIMIT = 62 * 1024 * 1024
LOG2E = 1.4426950408889634
F32 = jnp.float32
BF16 = jnp.bfloat16
ORDER = ((0, 0), (3, 0), (1, 0), (0, 3), (0, 1), (2, 0), (3, 3), (3, 1), (1, 3), (1, 1), (0, 2), (2, 3), (2, 1), (3, 2), (1, 2), (2, 2))


def main_kernel(
    owner_hbm, fill_hbm, q_hbm, span_hbm, cache_hbm, w_hbm, o_ref,
    owner_ref, fill_ref, q_ref, span_ref, cache_ref, table_v, table,
    send, sfill, recv, rfill, qs, m, acc, wfull, heads, gath, total, zout, obuf,
    in_s, kv_s, kv_r, f_s, f_r, w_s, w_r, a_s, a_r, g_s, g_r, b_s, b_r, o_s, o_r,
):
    g = lax.axis_index("grp")
    t = lax.axis_index("tp")
    x, y, c = g // (NY * NC), (g // NC) % NY, g % NC

    def at(px, py, pc):
        return (px % NX) * (NY * NC) + (py % NY) * NC + pc

    sib = at(x, y, 1 - c)

    def copy(src, dst, ssem, rsem, dev):
        return pltpu.make_async_remote_copy(
            src_ref=src, dst_ref=dst, send_sem=ssem, recv_sem=rsem, device_id=dev, device_id_type=MESH
        )

    barrier = pltpu.get_barrier_semaphore()

    def greet(s, k):
        pl.semaphore_signal(barrier, inc=1, device_id=((g + s) % GRP, t), device_id_type=MESH)
        return k

    lax.fori_loop(1, GRP, greet, 0)
    for s in range(1, NZ):
        pl.semaphore_signal(barrier, inc=1, device_id=(g, (t + s) % NZ), device_id_type=MESH)
    loads = [
        pltpu.make_async_copy(owner_hbm, owner_ref, in_s.at[0]),
        pltpu.make_async_copy(fill_hbm, fill_ref, in_s.at[1]),
        pltpu.make_async_copy(cache_hbm, cache_ref, in_s.at[2]),
        pltpu.make_async_copy(w_hbm, wfull.at[t], in_s.at[3]),
        pltpu.make_async_copy(q_hbm, q_ref, in_s.at[4]),
        pltpu.make_async_copy(span_hbm, span_ref, in_s.at[5]),
    ]
    for d in loads:
        d.start()

    loads[0].wait()
    loads[1].wait()
    slots = owner_ref.shape[1]
    shape = (GRP, slots)
    own = jnp.broadcast_to(owner_ref[...], shape)
    fill = jnp.broadcast_to(fill_ref[...], shape)
    block = lax.broadcasted_iota(jnp.int32, shape, 1)
    hit = own == lax.broadcasted_iota(jnp.int32, shape, 0)
    low = jnp.min(jnp.where(hit, block, slots), 1, keepdims=True)
    high = jnp.max(jnp.where(hit, block, -1), 1, keepdims=True)
    code = jnp.sum(jnp.where(hit, jnp.where(block == low, fill, fill * 256), 0), 1, keepdims=True)
    lane = lax.broadcasted_iota(jnp.int32, (GRP, KB), 1)
    table_v[...] = jnp.where(lane == 0, jnp.minimum(low, slots - 1), jnp.maximum(high, 0))
    sfill[...] = jnp.broadcast_to(code, (GRP, KB)).reshape(GRP, 1, KB)
    to_smem = pltpu.make_async_copy(table_v, table, in_s.at[6])
    to_smem.start()
    to_smem.wait()
    loads[2].wait()

    def load(dst):
        return cache_ref[table[dst, 0]], cache_ref[table[dst, 1]]

    def pack(s, k):
        dst = (g + s) % GRP
        first, second = load(dst)
        send[dst, :KB] = first
        send[dst, KB:] = second
        return k

    lax.fori_loop(1, GRP, pack, 0)
    first, second = load(g)
    recv[g, :KB] = first
    recv[g, KB:] = second
    rfill[g] = sfill[g]
    loads[3].wait()
    pl.semaphore_wait(barrier, GRP - 1 + NZ - 1)

    up, down = (t + 1) % NZ, (t + NZ - 1) % NZ
    half = WIDTH // 2

    def wcopy(n, z, lo, size, k, dev):
        part = wfull.at[z, pl.ds(lo, size)]
        return copy(part, part, w_s.at[n], w_r.at[z, k], (g, dev))

    wsends = [wcopy(0, t, 0, WIDTH, 0, up), wcopy(1, t, 0, WIDTH, 0, down)]
    for d in wsends:
        d.start()

    def wpass(j, lo, hi):
        low, high = (t + NZ - j) % NZ, (t + j) % NZ
        wcopy(0, low, 0, WIDTH, 0, up).wait_recv()
        d0 = wcopy(2 * j, low, lo, hi, 0, up)
        d0.start()
        wcopy(0, high, 0, WIDTH, 0, down).wait_recv()
        d1 = wcopy(2 * j + 1, high, half if hi < WIDTH else 0, hi, 1 if hi < WIDTH else 0, down)
        d1.start()
        wsends.extend([d0, d1])

    def where_to(s):
        o = (s * 11) % GRP
        return o // (NY * NC), (o // NC) % NY, o % NC

    def kv_copy(dst, s):
        return copy(send.at[dst], recv.at[g], kv_s.at[s], kv_r.at[g], (dst, t))

    def fill_copy(dst, s):
        return copy(sfill.at[dst], rfill.at[g], f_s.at[s], f_r.at[g], (dst, t))

    def give(s, k):
        dx, dy, dc = where_to(s)
        dst = at(x + dx, y + dy, (c + dc) % NC)
        kv_copy(dst, s).start()
        fill_copy(dst, s).start()
        return k

    lax.fori_loop(1, AHEAD + 1, give, 0)
    loads[4].wait()
    loads[5].wait()

    heads_n = WIDTH // HD
    for h in range(heads_n):
        qs[h * NEW:(h + 1) * NEW, :] = q_ref[:, h * HD:(h + 1) * HD]
    factor = LOG2E / HD**0.5
    blk = 256
    ones = jnp.ones((CAP * KB, HD), BF16)

    def scores(rows, keys):
        return lax.dot_general(qs[rows, :], keys, (((1,), (1,)), ((), ())), preferred_element_type=F32) * factor

    span_k, span_v = span_ref[:, :HD], span_ref[:, HD:]
    span_aug = jnp.concatenate([span_v, ones[:NEW]], 1)
    row = lax.broadcasted_iota(jnp.int32, (blk, NEW), 0) % NEW
    col = lax.broadcasted_iota(jnp.int32, (blk, NEW), 1)
    for qb in range(WIDTH // blk):
        rows = pl.ds(qb * blk, blk)
        s = jnp.where(col <= row, scores(rows, span_k), NEG)
        top = jnp.max(s, 1, keepdims=True)
        m[rows, :] = jnp.broadcast_to(top, (blk, HD))
        p = jnp.exp2(s - top).astype(BF16)
        acc[rows, :] = jnp.dot(p, span_aug, preferred_element_type=F32)

    lane = lax.broadcasted_iota(jnp.int32, (1, KB), 1)

    def attend(src):
        fills = rfill[src]
        bias = jnp.concatenate(
            [jnp.where(lane < fills % 256, 0.0, NEG), jnp.where(lane < fills // 256, 0.0, NEG)], 1
        )
        keys = recv[src, :, :HD]
        vals = jnp.concatenate([recv[src, :, HD:], ones], 1)
        for qb in range(WIDTH // blk):
            rows = pl.ds(qb * blk, blk)
            s = scores(rows, keys) + bias
            old = m[rows, :]
            new = jnp.maximum(old, jnp.max(s, 1, keepdims=True))
            alpha = jnp.exp2(old - new)
            p = jnp.exp2(s - jnp.concatenate([new, new], 1)).astype(BF16)
            part = jnp.dot(p, vals, preferred_element_type=F32)
            acc[rows, :] = acc[rows, :] * jnp.concatenate([alpha, alpha], 1) + part
            m[rows, :] = new

    attend(g)

    def take(s, k):
        dx, dy, dc = where_to(s)
        src = at(x + NX - dx, y + NY - dy, (c + dc) % NC)
        copy(send.at[src], recv.at[src], kv_s.at[s], kv_r.at[src], (src, t)).wait_recv()
        copy(sfill.at[src], rfill.at[src], f_s.at[s], f_r.at[src], (src, t)).wait_recv()
        attend(src)
        return k

    def take_give(s, k):
        give(s + AHEAD, k)
        return take(s, k)

    def run(lo, hi):
        split = min(max(GRP - AHEAD, lo), hi)
        if lo < split:
            lax.fori_loop(lo, split, take_give, 0)
        if split < hi:
            lax.fori_loop(split, hi, take, 0)

    run(1, STOPS[0])
    wpass(1, 0, WIDTH)
    run(STOPS[0], STOPS[1])
    wpass(2, 0, WIDTH)
    run(STOPS[1], STOPS[2])
    wpass(3, 0, half)
    total[...] = jnp.zeros_like(total)
    run(STOPS[2], GRP)

    per_half = heads_n // 2

    def zcopy(hf, s, dst):
        z = (t + s) % NZ
        return copy(heads.at[hf, z], gath.at[g, hf, dst(z)], a_s.at[hf, s], a_r.at[hf, dst(z)], (g, z))

    for hf in range(2):
        for h in range(per_half):
            rows = pl.ds((hf * per_half + h) * NEW, NEW)
            out = (acc[rows, :HD] / acc[rows, HD:]).astype(BF16)
            heads[hf, :, :, h * HD:(h + 1) * HD] = out.reshape(NZ, CHUNK, HD)
        for s in range(1, NZ):
            zcopy(hf, s, lambda z: t).start()
        gath[g, hf, t] = heads[hf, t]

    def spread_in(hf):
        for s in range(1, NZ):
            zcopy(hf, s, lambda z: z).wait_recv()

    sends = []

    def piece(owner, lo, size):
        return gath.at[owner, lo // NZ, pl.ds(lo % NZ, size)]

    def push(owner, lo, size, quarter, dev):
        part = piece(owner, lo, size)
        d = copy(part, part, g_s.at[len(sends)], g_r.at[owner, quarter], (dev, t))
        d.start()
        sends.append(d)

    def arrived(owner, lo, size, quarter):
        part = piece(owner, lo, size)
        copy(part, part, g_s.at[0], g_r.at[owner, quarter], (sib, t)).wait_recv()

    def place(h, d1, d2, pc):
        return at(x + d1, y + d2, pc) if h == 0 else at(x + d2, y + d1, pc)

    def share(h, owner):
        part = piece(owner, NZ * h, NZ)
        d = copy(part, part, b_s.at[len(shared)], b_r.at[owner, h], (sib, t))
        d.start()
        shared.append(d)

    shared = []

    def event(h, d1, d2):
        owner = place(h, d1, d2, c)
        lo = NZ * h
        q = 2 * h
        fwd1, back1 = place(h, 1, 0, c), place(h, 3, 0, c)
        fwd2, back2 = place(h, 0, 1, c), place(h, 0, 3, c)
        last = d2 if d2 else d1
        if last == 2:
            arrived(owner, lo, 4, q)
            arrived(owner, lo + 4, 4, q + 1)
        elif last:
            arrived(owner, lo, NZ, q)
        if d2 == 0:
            if d1 == 0:
                push(owner, lo, NZ, q, fwd1)
                push(owner, lo, NZ, q, back1)
            elif d1 == 3:
                push(owner, lo, 4, q, fwd1)
            elif d1 == 1:
                push(owner, lo + 4, 4, q + 1, back1)
            push(owner, lo, NZ, q, fwd2)
            push(owner, lo, NZ, q, back2)
        elif d2 == 3:
            push(owner, lo, 4, q, fwd2)
        elif d2 == 1:
            push(owner, lo + 4, 4, q + 1, back2)
        share(h, owner)

    def multiply(h, d2):
        owners = [place(h, d1, d2, pc) for d1 in range(4) for pc in range(2)]
        for d1 in range(4):
            other = place(h, d1, d2, 1 - c)
            part = piece(other, NZ * h, NZ)
            copy(part, part, b_s.at[0], b_r.at[other, h], (sib, t)).wait_recv()

        def step(z, sum_):
            rows = jnp.concatenate([gath[o, h, z] for o in owners], 0)
            return sum_ + jnp.dot(rows, wfull[z, h * half:(h + 1) * half], preferred_element_type=F32)

        got = lax.fori_loop(0, NZ, step, jnp.zeros((len(owners) * CHUNK, FEAT), F32))
        for i, o in enumerate(owners):
            total[o] = total[o] + got[i * CHUNK:(i + 1) * CHUNK]

    def ocopy(s, e, dst):
        z = (t + s) % NZ
        to = dst(z)
        here = z * 4 + e * 2 if to is t else t * 4 + e * 2
        return copy(
            zout.at[pl.ds(here, 2)], obuf.at[pl.ds(e * 2, 2), to], o_s.at[s, e], o_r.at[to, e], (g, z)
        )

    def hand(late):
        for s in range(1, NZ):
            z = (t + s) % NZ
            for e in range(2):
                far = ((z // 2 + NX - x) % NX == 2) | (((z % 2) * 2 + e + NY - y) % NY == 2)

                @pl.when(far if late else jnp.logical_not(far))
                def _():
                    ocopy(s, e, lambda z: t).start()

    for n, (d1, d2) in enumerate(ORDER):
        for h in range(2):
            if n == 0:
                spread_in(h)
            event(h, d1, d2)
        if n == 5:
            opposite = (t + 4) % NZ
            wcopy(0, opposite, 0, half, 0, up).wait_recv()
            wcopy(0, opposite, half, half, 1, down).wait_recv()
        if n in (6, 7):
            multiply(n - 6, 0)
        if n == 12:
            for h in range(2):
                multiply(h, 3)
                multiply(h, 1)
            zout[...] = total[...].astype(BF16)
            hand(False)
    for h in range(2):
        multiply(h, 2)

    def finish(o):
        zout[o] = total[o].astype(BF16)

    for i in range(NX):
        for pc in range(NC):
            finish(at(x + 2, i, pc))
            if i:
                finish(at(x + 2 + i, y + 2, pc))
    hand(True)
    obuf[:, t] = zout[pl.ds(t * 4, 4)]
    for s in range(1, NZ):
        for e in range(2):
            ocopy(s, e, lambda z: z).wait_recv()
    o_ref[...] = obuf[...]

    def sent(s, k):
        dx, dy, dc = where_to(s)
        dst = at(x + dx, y + dy, (c + dc) % NC)
        kv_copy(dst, s).wait_send()
        fill_copy(dst, s).wait_send()
        return k

    lax.fori_loop(1, GRP, sent, 0)

    for s in range(1, NZ):
        for e in range(2):
            zcopy(e, s, lambda z: t).wait_send()
            ocopy(s, e, lambda z: t).wait_send()
    for d in wsends + sends + shared:
        d.wait_send()


def body(queries, span_kv, cache, block_owner, block_fill, out_weight):
    slots = cache.shape[0]
    any_ = pl.BlockSpec(memory_space=pl.ANY)
    vmem = pl.BlockSpec(memory_space=pltpu.VMEM)
    dma = pltpu.SemaphoreType.DMA
    out = pl.pallas_call(
        main_kernel,
        out_shape=jax.ShapeDtypeStruct((GRP // NZ, NZ, CHUNK, FEAT), BF16),
        in_specs=[any_] * 6,
        out_specs=vmem,
        scratch_shapes=[
            pltpu.VMEM((1, slots), jnp.int32),
            pltpu.VMEM((1, slots), jnp.int32),
            pltpu.VMEM((NEW, WIDTH), BF16),
            pltpu.VMEM((NEW, 2 * HD), BF16),
            pltpu.VMEM((slots, KB, 2 * HD), BF16),
            pltpu.VMEM((GRP, KB), jnp.int32),
            pltpu.SMEM((GRP, KB), jnp.int32),
            pltpu.VMEM((GRP, CAP * KB, 2 * HD), BF16),
            pltpu.VMEM((GRP, 1, KB), jnp.int32),
            pltpu.VMEM((GRP, CAP * KB, 2 * HD), BF16),
            pltpu.VMEM((GRP, 1, KB), jnp.int32),
            pltpu.VMEM((WIDTH, HD), BF16),
            pltpu.VMEM((WIDTH, HD), F32),
            pltpu.VMEM((WIDTH, 2 * HD), F32),
            pltpu.VMEM((NZ, WIDTH, FEAT), BF16),
            pltpu.VMEM((2, NZ, CHUNK, WIDTH // 2), BF16),
            pltpu.VMEM((GRP, 2, NZ, CHUNK, WIDTH // 2), BF16),
            pltpu.VMEM((GRP, CHUNK, FEAT), F32),
            pltpu.VMEM((GRP, CHUNK, FEAT), BF16),
            pltpu.VMEM((GRP // NZ, NZ, CHUNK, FEAT), BF16),
            dma((7,)),
            dma((GRP,)), dma((GRP,)), dma((GRP,)), dma((GRP,)),
            dma((NZ,)), dma((NZ, 2)),
            dma((2, NZ)), dma((2, NZ)),
            dma((40,)), dma((GRP, 4)),
            dma((32,)), dma((GRP, 2)),
            dma((NZ, 2)), dma((NZ, 2)),
        ],
        compiler_params=pltpu.CompilerParams(
            collective_id=0, has_side_effects=True, vmem_limit_bytes=VMEM_LIMIT
        ),
    )(
        block_owner.reshape(1, slots),
        block_fill.reshape(1, slots),
        queries.reshape(NEW, WIDTH),
        span_kv.reshape(NEW, 2 * HD),
        cache.reshape(slots, KB, 2 * HD),
        out_weight,
    )
    return out.reshape(GRP // NZ * NEW, FEAT)


def solution(mesh):
    in_specs = (
        P("grp", None, "tp"),
        P("grp", None, "tp", None),
        P("grp", None, "tp", None),
        P("grp", None),
        P("grp", None),
        P("tp", "grp"),
    )
    out_specs = P("tp", "grp")
    return jax.shard_map(body, mesh=mesh, in_specs=in_specs, out_specs=out_specs, check_vma=False)
```

```python
import functools

import jax
import jax.numpy as jnp
from jax import lax
from jax.experimental import pallas as pl
from jax.experimental.pallas import tpu as pltpu
from jax.sharding import PartitionSpec as P

MESH = pl.DeviceIdType.MESH
NX, NY, NC, NZ = 4, 4, 2, 8
CHIPS = NX * NY
GRP = CHIPS * NC
CAP = 2
KB = 128
HD = 128
NEW = 128
WIDTH = 1024
FEAT = 256
CHUNK = NEW // NZ
NEG = -1e30
EARLY = 12
SWITCH = 20
VMEM_LIMIT = 62 * 1024 * 1024
LOG2E = 1.4426950408889634
F32 = jnp.float32
BF16 = jnp.bfloat16
ORDER = ((0, 0), (3, 0), (1, 0), (0, 3), (0, 1), (2, 0), (3, 3), (3, 1), (1, 3), (1, 1), (0, 2), (2, 3), (2, 1), (3, 2), (1, 2), (2, 2))


def main_kernel(
    owner_hbm, fill_hbm, q_hbm, span_hbm, cache_hbm, w_hbm, o_ref,
    owner_ref, fill_ref, q_ref, span_ref, cache_ref, table_v, table,
    send, sfill, recv, rfill, qs, m, acc, wfull, heads, gath, total, zout, obuf,
    in_s, kv_s, kv_r, f_s, f_r, w_s, w_r, a_s, a_r, g_s, g_r, b_s, b_r, o_s, o_r,
):
    g = lax.axis_index("grp")
    t = lax.axis_index("tp")
    x, y, c = g // (NY * NC), (g // NC) % NY, g % NC

    def at(px, py, pc):
        return (px % NX) * (NY * NC) + (py % NY) * NC + pc

    sib = at(x, y, 1 - c)

    def copy(src, dst, ssem, rsem, dev):
        return pltpu.make_async_remote_copy(
            src_ref=src, dst_ref=dst, send_sem=ssem, recv_sem=rsem, device_id=dev, device_id_type=MESH
        )

    barrier = pltpu.get_barrier_semaphore()

    def greet(s, k):
        pl.semaphore_signal(barrier, inc=1, device_id=((g + s) % GRP, t), device_id_type=MESH)
        return k

    lax.fori_loop(1, GRP, greet, 0)
    for s in range(1, NZ):
        pl.semaphore_signal(barrier, inc=1, device_id=(g, (t + s) % NZ), device_id_type=MESH)
    loads = [
        pltpu.make_async_copy(owner_hbm, owner_ref, in_s.at[0]),
        pltpu.make_async_copy(fill_hbm, fill_ref, in_s.at[1]),
        pltpu.make_async_copy(cache_hbm, cache_ref, in_s.at[2]),
        pltpu.make_async_copy(w_hbm, wfull.at[t], in_s.at[3]),
        pltpu.make_async_copy(q_hbm, q_ref, in_s.at[4]),
        pltpu.make_async_copy(span_hbm, span_ref, in_s.at[5]),
    ]
    for d in loads:
        d.start()

    loads[0].wait()
    loads[1].wait()
    slots = owner_ref.shape[1]
    shape = (GRP, slots)
    own = jnp.broadcast_to(owner_ref[...], shape)
    fill = jnp.broadcast_to(fill_ref[...], shape)
    block = lax.broadcasted_iota(jnp.int32, shape, 1)
    hit = own == lax.broadcasted_iota(jnp.int32, shape, 0)
    low = jnp.min(jnp.where(hit, block, slots), 1, keepdims=True)
    high = jnp.max(jnp.where(hit, block, -1), 1, keepdims=True)
    code = jnp.sum(jnp.where(hit, jnp.where(block == low, fill, fill * 256), 0), 1, keepdims=True)
    lane = lax.broadcasted_iota(jnp.int32, (GRP, KB), 1)
    table_v[...] = jnp.where(lane == 0, jnp.minimum(low, slots - 1), jnp.maximum(high, 0))
    sfill[...] = jnp.broadcast_to(code, (GRP, KB)).reshape(GRP, 1, KB)
    to_smem = pltpu.make_async_copy(table_v, table, in_s.at[6])
    to_smem.start()
    to_smem.wait()
    loads[2].wait()

    def load(dst):
        return cache_ref[table[dst, 0]], cache_ref[table[dst, 1]]

    def pack(s, k):
        dst = (g + s) % GRP
        first, second = load(dst)
        send[dst, :KB] = first
        send[dst, KB:] = second
        return k

    lax.fori_loop(1, GRP, pack, 0)
    first, second = load(g)
    recv[g, :KB] = first
    recv[g, KB:] = second
    rfill[g] = sfill[g]
    loads[3].wait()
    pl.semaphore_wait(barrier, GRP - 1 + NZ - 1)

    up, down = (t + 1) % NZ, (t + NZ - 1) % NZ
    half = WIDTH // 2

    def wcopy(n, z, lo, size, k, dev):
        part = wfull.at[z, pl.ds(lo, size)]
        return copy(part, part, w_s.at[n], w_r.at[z, k], (g, dev))

    WSENDS = [
        (0, 0, 0, WIDTH, 0, 1), (1, 0, 0, WIDTH, 0, -1), (2, -1, 0, WIDTH, 0, 1), (3, 1, 0, WIDTH, 0, -1),
        (4, -2, 0, WIDTH, 0, 1), (5, 2, 0, WIDTH, 0, -1), (6, -3, 0, half, 0, 1), (7, 3, half, half, 1, -1),
    ]

    def wsend(n):
        n, dz, lo, size, k, way = WSENDS[n]
        return wcopy(n, (t + NZ + dz) % NZ, lo, size, k, up if way == 1 else down)

    wsend(0).start()
    wsend(1).start()

    def wpass(j):
        wcopy(0, (t + NZ - j) % NZ, 0, WIDTH, 0, up).wait_recv()
        wsend(2 * j).start()
        wcopy(0, (t + j) % NZ, 0, WIDTH, 0, down).wait_recv()
        wsend(2 * j + 1).start()

    def wlast():
        opposite = (t + 4) % NZ
        wcopy(0, opposite, 0, half, 0, up).wait_recv()
        wcopy(0, opposite, half, half, 1, down).wait_recv()

    def hop(k):
        o = (k * 5) % CHIPS
        return o // NY, o % NY

    def kv_copies(dst, n):
        return (
            copy(send.at[dst], recv.at[g], kv_s.at[n], kv_r.at[g], (dst, t)),
            copy(sfill.at[dst], rfill.at[g], f_s.at[n], f_r.at[g], (dst, t)),
        )

    def give_to(p, k):
        dx, dy = hop(k)
        return kv_copies(at(x + dx, y + dy, p), p * CHIPS + k)

    def give(p, k, carry):
        for d in give_to(p, k):
            d.start()
        return carry

    for d in kv_copies(sib, 0):
        d.start()
    lax.fori_loop(1, CHIPS, functools.partial(give, 0), 0)

    def more():
        def done(k, carry):
            for d in give_to(0, k):
                d.wait_send()
            return carry

        lax.fori_loop(1, EARLY + 1, done, 0)
        lax.fori_loop(1, CHIPS, functools.partial(give, 1), 0)

    loads[4].wait()
    loads[5].wait()

    heads_n = WIDTH // HD
    for h in range(heads_n):
        qs[h * NEW:(h + 1) * NEW, :] = q_ref[:, h * HD:(h + 1) * HD]
    factor = LOG2E / HD**0.5
    blk = 256
    ones = jnp.ones((CAP * KB, HD), BF16)

    def scores(rows, keys):
        return lax.dot_general(qs[rows, :], keys, (((1,), (1,)), ((), ())), preferred_element_type=F32) * factor

    span_k, span_v = span_ref[:, :HD], span_ref[:, HD:]
    span_aug = jnp.concatenate([span_v, ones[:NEW]], 1)
    row = lax.broadcasted_iota(jnp.int32, (blk, NEW), 0) % NEW
    col = lax.broadcasted_iota(jnp.int32, (blk, NEW), 1)
    for qb in range(WIDTH // blk):
        rows = pl.ds(qb * blk, blk)
        s = jnp.where(col <= row, scores(rows, span_k), NEG)
        top = jnp.max(s, 1, keepdims=True)
        m[rows, :] = jnp.broadcast_to(top, (blk, HD))
        p = jnp.exp2(s - top).astype(BF16)
        acc[rows, :] = jnp.dot(p, span_aug, preferred_element_type=F32)

    lane = lax.broadcasted_iota(jnp.int32, (1, KB), 1)

    def attend(src):
        fills = rfill[src]
        bias = jnp.concatenate(
            [jnp.where(lane < fills % 256, 0.0, NEG), jnp.where(lane < fills // 256, 0.0, NEG)], 1
        )
        keys = recv[src, :, :HD]
        vals = jnp.concatenate([recv[src, :, HD:], ones], 1)
        for qb in range(WIDTH // blk):
            rows = pl.ds(qb * blk, blk)
            s = scores(rows, keys) + bias
            old = m[rows, :]
            new = jnp.maximum(old, jnp.max(s, 1, keepdims=True))
            alpha = jnp.exp2(old - new)
            p = jnp.exp2(s - jnp.concatenate([new, new], 1)).astype(BF16)
            part = jnp.dot(p, vals, preferred_element_type=F32)
            acc[rows, :] = acc[rows, :] * jnp.concatenate([alpha, alpha], 1) + part
            m[rows, :] = new

    def take_from(src):
        for d in (
            copy(send.at[src], recv.at[src], kv_s.at[0], kv_r.at[src], (src, t)),
            copy(sfill.at[src], rfill.at[src], f_s.at[0], f_r.at[src], (src, t)),
        ):
            d.wait_recv()
        attend(src)

    def take(i, k):
        dx, dy = hop(i // NC)
        take_from(at(x + NX - dx, y + NY - dy, i % NC))
        return k

    def run(lo, hi):
        lax.fori_loop(lo, hi, take, 0)

    attend(g)
    take_from(sib)
    total[...] = jnp.zeros_like(total)

    per_half = heads_n // 2

    def zcopy(hf, s, dst):
        z = (t + s) % NZ
        return copy(heads.at[hf, z], gath.at[g, hf, dst(z)], a_s.at[hf, s], a_r.at[hf, dst(z)], (g, z))

    def spread(hf):
        for s in range(1, NZ):
            zcopy(hf, s, lambda z: t).start()
        gath[g, hf, t] = heads[hf, t]

    def finalize():
        for hf in range(2):
            for h in range(per_half):
                rows = pl.ds((hf * per_half + h) * NEW, NEW)
                out = (acc[rows, :HD] / acc[rows, HD:]).astype(BF16)
                heads[hf, :, :, h * HD:(h + 1) * HD] = out.reshape(NZ, CHUNK, HD)
            if hf == 0:
                spread(0)

    def spread_in(hf):
        for s in range(1, NZ):
            zcopy(hf, s, lambda z: z).wait_recv()

    def piece(owner, lo, size):
        return gath.at[owner, lo // NZ, pl.ds(lo % NZ, size)]

    def arrived(owner, lo, size, quarter):
        part = piece(owner, lo, size)
        copy(part, part, g_s.at[0], g_r.at[owner, quarter], (sib, t)).wait_recv()

    def place(h, d1, d2, pc):
        return at(x + d1, y + d2, pc) if h == 0 else at(x + d2, y + d1, pc)

    PUSHES = {
        (0, 0): [((1, 0), 0, NZ, 0), ((3, 0), 0, NZ, 0), ((0, 1), 0, NZ, 0), ((0, 3), 0, NZ, 0)],
        (3, 0): [((1, 0), 0, 4, 0), ((0, 1), 0, NZ, 0), ((0, 3), 0, NZ, 0)],
        (1, 0): [((3, 0), 4, 4, 1), ((0, 1), 0, NZ, 0), ((0, 3), 0, NZ, 0)],
        (2, 0): [((0, 1), 0, NZ, 0), ((0, 3), 0, NZ, 0)],
    }
    for d1 in range(4):
        PUSHES[(d1, 3)] = [((0, 1), 0, 4, 0)]
        PUSHES[(d1, 1)] = [((0, 3), 4, 4, 1)]
    first_sem, count = {}, 0
    for h in range(2):
        for d in ORDER:
            first_sem[(h, d)] = count
            count += len(PUSHES.get(d, ()))

    def pushes(h, d1, d2):
        owner = place(h, d1, d2, c)
        base = first_sem[(h, (d1, d2))]
        out = []
        for i, (to, lo, size, quarter) in enumerate(PUSHES.get((d1, d2), ())):
            part = piece(owner, NZ * h + lo, size)
            dev = place(h, to[0], to[1], c)
            out.append(copy(part, part, g_s.at[base + i], g_r.at[owner, 2 * h + quarter], (dev, t)))
        return out

    def share(h, d1, d2):
        owner = place(h, d1, d2, c)
        part = piece(owner, NZ * h, NZ)
        n = h * CHIPS + ORDER.index((d1, d2))
        return copy(part, part, b_s.at[n], b_r.at[owner, h], (sib, t))

    def event(h, d1, d2):
        owner = place(h, d1, d2, c)
        lo = NZ * h
        q = 2 * h
        last = d2 if d2 else d1
        if last == 2:
            arrived(owner, lo, 4, q)
            arrived(owner, lo + 4, 4, q + 1)
        elif last:
            arrived(owner, lo, NZ, q)
        for d in pushes(h, d1, d2):
            d.start()
        share(h, d1, d2).start()

    def shared_in(h, groups):
        for d2 in groups:
            for d1 in range(4):
                other = place(h, d1, d2, 1 - c)
                part = piece(other, NZ * h, NZ)
                copy(part, part, b_s.at[0], b_r.at[other, h], (sib, t)).wait_recv()

    def multiply(h, groups, *pcs):
        owners = [place(h, d1, d2, pc) for pc in pcs for d2 in groups for d1 in range(4)]
        rows = jnp.concatenate(
            [jnp.concatenate([gath[o, h, z] for o in owners], 0) for z in range(NZ)], 1
        )
        weights = wfull[:, h * half:(h + 1) * half].reshape(NZ * half, FEAT)
        got = jnp.dot(rows, weights, preferred_element_type=F32)
        for i, o in enumerate(owners):
            total[o] = total[o] + got[i * CHUNK:(i + 1) * CHUNK]

    def ocopy(s, e, pc, dst):
        z = (t + s) % NZ
        to = dst(z)
        here = z * 4 + e * 2 + pc if to is t else t * 4 + e * 2 + pc
        return copy(zout.at[here], obuf.at[e * 2 + pc, to], o_s.at[s, e, pc], o_r.at[to, e, pc], (g, z))

    def hand(pc, late):
        for s in range(1, NZ):
            z = (t + s) % NZ
            for e in range(2):
                if late is None:
                    ocopy(s, e, pc, lambda z: t).start()
                    continue
                far = ((z // 2 + NX - x) % NX == 2) | (((z % 2) * 2 + e + NY - y) % NY == 2)

                @pl.when(far if late else jnp.logical_not(far))
                def _():
                    ocopy(s, e, pc, lambda z: t).start()

    def finish(pc, late):
        for d1 in range(4):
            for d2 in range(4):
                if late is None or late == (d1 == 2 or d2 == 2):
                    o = at(x + d1, y + d2, pc)
                    zout[o] = total[o].astype(BF16)
        hand(pc, late)

    near = (0, 3, 1)
    every = (0, 3, 1, 2)

    def events(lo, hi):
        for d in ORDER[lo:hi]:
            for h in range(2):
                event(h, *d)

    def opening():
        finalize()
        spread(1)
        spread_in(0)
        event(0, 0, 0)
        spread_in(1)
        event(1, 0, 0)

    @pl.when(c == 0)
    def _():
        wpass(1)
        run(2, 12)
        wpass(2)
        run(12, 20)
        more()
        run(20, GRP)
        opening()
        events(1, 5)
        wpass(3)
        events(5, 16)
        wlast()
        for h in range(2):
            multiply(h, every, 0)
        finish(0, None)
        for h in range(2):
            shared_in(h, near)
            multiply(h, near, 1)
        finish(1, False)
        for h in range(2):
            shared_in(h, (2,))
            multiply(h, (2,), 1)

    @pl.when(c == 1)
    def _():
        wpass(1)
        wpass(2)
        more()
        run(2, 10)
        wpass(3)
        run(10, GRP)
        opening()
        events(1, 4)
        wlast()
        shared_in(0, every)
        multiply(0, every, 0)
        events(4, 8)
        shared_in(1, every)
        multiply(1, every, 0)
        events(8, 13)
        finish(0, None)
        multiply(0, near, 1)
        events(13, 14)
        multiply(1, near, 1)
        events(14, 16)
        finish(1, False)
        for h in range(2):
            multiply(h, (2,), 1)

    finish(1, True)
    obuf[:, t] = zout[pl.ds(t * 4, 4)]
    for s in range(1, NZ):
        for e in range(2):
            for pc in range(NC):
                ocopy(s, e, pc, lambda z: z).wait_recv()
    o_ref[...] = obuf[...]

    for d in kv_copies(sib, 0):
        d.wait_send()

    def sent(p, k, carry):
        for d in give_to(p, k):
            d.wait_send()
        return carry

    lax.fori_loop(EARLY + 1, CHIPS, functools.partial(sent, 0), 0)
    lax.fori_loop(1, CHIPS, functools.partial(sent, 1), 0)
    for s in range(1, NZ):
        for e in range(2):
            zcopy(e, s, lambda z: t).wait_send()
            for pc in range(NC):
                ocopy(s, e, pc, lambda z: t).wait_send()
    for n in range(NZ):
        wsend(n).wait_send()
    for h in range(2):
        for d in ORDER:
            share(h, *d).wait_send()
            for p in pushes(h, *d):
                p.wait_send()


def body(queries, span_kv, cache, block_owner, block_fill, out_weight):
    slots = cache.shape[0]
    any_ = pl.BlockSpec(memory_space=pl.ANY)
    vmem = pl.BlockSpec(memory_space=pltpu.VMEM)
    dma = pltpu.SemaphoreType.DMA
    out = pl.pallas_call(
        main_kernel,
        out_shape=jax.ShapeDtypeStruct((GRP // NZ, NZ, CHUNK, FEAT), BF16),
        in_specs=[any_] * 6,
        out_specs=vmem,
        scratch_shapes=[
            pltpu.VMEM((1, slots), jnp.int32),
            pltpu.VMEM((1, slots), jnp.int32),
            pltpu.VMEM((NEW, WIDTH), BF16),
            pltpu.VMEM((NEW, 2 * HD), BF16),
            pltpu.VMEM((slots, KB, 2 * HD), BF16),
            pltpu.VMEM((GRP, KB), jnp.int32),
            pltpu.SMEM((GRP, KB), jnp.int32),
            pltpu.VMEM((GRP, CAP * KB, 2 * HD), BF16),
            pltpu.VMEM((GRP, 1, KB), jnp.int32),
            pltpu.VMEM((GRP, CAP * KB, 2 * HD), BF16),
            pltpu.VMEM((GRP, 1, KB), jnp.int32),
            pltpu.VMEM((WIDTH, HD), BF16),
            pltpu.VMEM((WIDTH, HD), F32),
            pltpu.VMEM((WIDTH, 2 * HD), F32),
            pltpu.VMEM((NZ, WIDTH, FEAT), BF16),
            pltpu.VMEM((2, NZ, CHUNK, WIDTH // 2), BF16),
            pltpu.VMEM((GRP, 2, NZ, CHUNK, WIDTH // 2), BF16),
            pltpu.VMEM((GRP, CHUNK, FEAT), F32),
            pltpu.VMEM((GRP, CHUNK, FEAT), BF16),
            pltpu.VMEM((GRP // NZ, NZ, CHUNK, FEAT), BF16),
            dma((7,)),
            dma((GRP,)), dma((GRP,)), dma((GRP,)), dma((GRP,)),
            dma((NZ,)), dma((NZ, 2)),
            dma((2, NZ)), dma((2, NZ)),
            dma((40,)), dma((GRP, 4)),
            dma((32,)), dma((GRP, 2)),
            dma((NZ, 2, NC)), dma((NZ, 2, NC)),
        ],
        compiler_params=pltpu.CompilerParams(
            collective_id=0, has_side_effects=True, vmem_limit_bytes=VMEM_LIMIT
        ),
    )(
        block_owner.reshape(1, slots),
        block_fill.reshape(1, slots),
        queries.reshape(NEW, WIDTH),
        span_kv.reshape(NEW, 2 * HD),
        cache.reshape(slots, KB, 2 * HD),
        out_weight,
    )
    return out.reshape(GRP // NZ * NEW, FEAT)


def solution(mesh):
    in_specs = (
        P("grp", None, "tp"),
        P("grp", None, "tp", None),
        P("grp", None, "tp", None),
        P("grp", None),
        P("grp", None),
        P("tp", "grp"),
    )
    out_specs = P("tp", "grp")
    return jax.shard_map(body, mesh=mesh, in_specs=in_specs, out_specs=out_specs, check_vma=False)
```

```python
import functools

import jax
import jax.numpy as jnp
from jax import lax
from jax.experimental import pallas as pl
from jax.experimental.pallas import tpu as pltpu
from jax.sharding import PartitionSpec as P

MESH = pl.DeviceIdType.MESH
NX, NY, NC, NZ = 4, 4, 2, 8
CHIPS = NX * NY
GRP = CHIPS * NC
CAP = 2
KB = 128
HD = 128
NEW = 128
WIDTH = 1024
FEAT = 256
CHUNK = NEW // NZ
NEG = -1e30
EARLY = 12
SWITCH = 20
VMEM_LIMIT = 62 * 1024 * 1024
LOG2E = 1.4426950408889634
F32 = jnp.float32
BF16 = jnp.bfloat16
ORDER = ((0, 0), (3, 0), (1, 0), (0, 3), (0, 1), (2, 0), (3, 3), (3, 1), (1, 3), (1, 1), (0, 2), (2, 3), (2, 1), (3, 2), (1, 2), (2, 2))


def main_kernel(
    owner_hbm, fill_hbm, q_hbm, span_hbm, cache_hbm, w_hbm, o_ref,
    owner_ref, fill_ref, q_ref, span_ref, cache_ref, table_v, table,
    send, sfill, recv, rfill, qs, m, acc, wfull, heads, gath, total, zout, obuf,
    in_s, kv_s, kv_r, f_s, f_r, w_s, w_r, a_s, a_r, g_s, g_r, b_s, b_r, o_s, o_r,
):
    g = lax.axis_index("grp")
    t = lax.axis_index("tp")
    x, y, c = g // (NY * NC), (g // NC) % NY, g % NC

    def at(px, py, pc):
        return (px % NX) * (NY * NC) + (py % NY) * NC + pc

    sib = at(x, y, 1 - c)

    def copy(src, dst, ssem, rsem, dev):
        return pltpu.make_async_remote_copy(
            src_ref=src, dst_ref=dst, send_sem=ssem, recv_sem=rsem, device_id=dev, device_id_type=MESH
        )

    barrier = pltpu.get_barrier_semaphore()

    def greet(s, k):
        pl.semaphore_signal(barrier, inc=1, device_id=((g + s) % GRP, t), device_id_type=MESH)
        return k

    lax.fori_loop(1, GRP, greet, 0)
    for s in range(1, NZ):
        pl.semaphore_signal(barrier, inc=1, device_id=(g, (t + s) % NZ), device_id_type=MESH)
    loads = [
        pltpu.make_async_copy(owner_hbm, owner_ref, in_s.at[0]),
        pltpu.make_async_copy(fill_hbm, fill_ref, in_s.at[1]),
        pltpu.make_async_copy(cache_hbm, cache_ref, in_s.at[2]),
        pltpu.make_async_copy(w_hbm, wfull.at[t], in_s.at[3]),
        pltpu.make_async_copy(q_hbm, q_ref, in_s.at[4]),
        pltpu.make_async_copy(span_hbm, span_ref, in_s.at[5]),
    ]
    for d in loads:
        d.start()

    loads[0].wait()
    loads[1].wait()
    slots = owner_ref.shape[1]
    shape = (GRP, slots)
    own = jnp.broadcast_to(owner_ref[...], shape)
    fill = jnp.broadcast_to(fill_ref[...], shape)
    block = lax.broadcasted_iota(jnp.int32, shape, 1)
    hit = own == lax.broadcasted_iota(jnp.int32, shape, 0)
    low = jnp.min(jnp.where(hit, block, slots), 1, keepdims=True)
    high = jnp.max(jnp.where(hit, block, -1), 1, keepdims=True)
    code = jnp.sum(jnp.where(hit, jnp.where(block == low, fill, fill * 256), 0), 1, keepdims=True)
    lane = lax.broadcasted_iota(jnp.int32, (GRP, KB), 1)
    table_v[...] = jnp.where(lane == 0, jnp.minimum(low, slots - 1), jnp.maximum(high, 0))
    sfill[...] = jnp.broadcast_to(code, (GRP, KB)).reshape(GRP, 1, KB)
    to_smem = pltpu.make_async_copy(table_v, table, in_s.at[6])
    to_smem.start()
    to_smem.wait()
    loads[2].wait()

    def load(dst):
        return cache_ref[table[dst, 0]], cache_ref[table[dst, 1]]

    def pack(s, k):
        dst = (g + s) % GRP
        first, second = load(dst)
        send[dst, :KB] = first
        send[dst, KB:] = second
        return k

    lax.fori_loop(1, GRP, pack, 0)
    first, second = load(g)
    recv[g, :KB] = first
    recv[g, KB:] = second
    rfill[g] = sfill[g]
    loads[3].wait()
    pl.semaphore_wait(barrier, GRP - 1 + NZ - 1)

    up, down = (t + 1) % NZ, (t + NZ - 1) % NZ
    half = WIDTH // 2

    def wcopy(n, z, lo, size, k, dev):
        part = wfull.at[z, pl.ds(lo, size)]
        return copy(part, part, w_s.at[n], w_r.at[z, k], (g, dev))

    WSENDS = [
        (0, 0, 0, WIDTH, 0, 1), (1, 0, 0, WIDTH, 0, -1), (2, -1, 0, WIDTH, 0, 1), (3, 1, 0, WIDTH, 0, -1),
        (4, -2, 0, WIDTH, 0, 1), (5, 2, 0, WIDTH, 0, -1), (6, -3, 0, half, 0, 1), (7, 3, half, half, 1, -1),
    ]

    def wsend(n):
        n, dz, lo, size, k, way = WSENDS[n]
        return wcopy(n, (t + NZ + dz) % NZ, lo, size, k, up if way == 1 else down)

    wsend(0).start()
    wsend(1).start()

    def wpass(j):
        wcopy(0, (t + NZ - j) % NZ, 0, WIDTH, 0, up).wait_recv()
        wsend(2 * j).start()
        wcopy(0, (t + j) % NZ, 0, WIDTH, 0, down).wait_recv()
        wsend(2 * j + 1).start()

    def wlast():
        opposite = (t + 4) % NZ
        wcopy(0, opposite, 0, half, 0, up).wait_recv()
        wcopy(0, opposite, half, half, 1, down).wait_recv()

    def hop(k):
        o = (k * 5) % CHIPS
        return o // NY, o % NY

    def kv_copies(dst, n):
        return (
            copy(send.at[dst], recv.at[g], kv_s.at[n], kv_r.at[g], (dst, t)),
            copy(sfill.at[dst], rfill.at[g], f_s.at[n], f_r.at[g], (dst, t)),
        )

    def give_to(p, k):
        dx, dy = hop(k)
        return kv_copies(at(x + dx, y + dy, p), p * CHIPS + k)

    def give(p, k, carry):
        for d in give_to(p, k):
            d.start()
        return carry

    for d in kv_copies(sib, 0):
        d.start()
    lax.fori_loop(1, CHIPS, functools.partial(give, 0), 0)

    def more():
        def done(k, carry):
            for d in give_to(0, k):
                d.wait_send()
            return carry

        lax.fori_loop(1, EARLY + 1, done, 0)
        lax.fori_loop(1, CHIPS, functools.partial(give, 1), 0)

    loads[4].wait()
    loads[5].wait()

    heads_n = WIDTH // HD
    for h in range(heads_n):
        qs[h * NEW:(h + 1) * NEW, :] = q_ref[:, h * HD:(h + 1) * HD]
    factor = LOG2E / HD**0.5
    blk = 256
    ones = jnp.ones((CAP * KB, HD), BF16)

    def scores(rows, keys):
        return lax.dot_general(qs[rows, :], keys, (((1,), (1,)), ((), ())), preferred_element_type=F32) * factor

    span_k, span_v = span_ref[:, :HD], span_ref[:, HD:]
    span_aug = jnp.concatenate([span_v, ones[:NEW]], 1)
    row = lax.broadcasted_iota(jnp.int32, (blk, NEW), 0) % NEW
    col = lax.broadcasted_iota(jnp.int32, (blk, NEW), 1)
    for qb in range(WIDTH // blk):
        rows = pl.ds(qb * blk, blk)
        s = jnp.where(col <= row, scores(rows, span_k), NEG)
        top = jnp.max(s, 1, keepdims=True)
        m[rows, :] = jnp.broadcast_to(top, (blk, HD))
        p = jnp.exp2(s - top).astype(BF16)
        acc[rows, :] = jnp.dot(p, span_aug, preferred_element_type=F32)

    lane = lax.broadcasted_iota(jnp.int32, (1, KB), 1)

    def attend(src):
        fills = rfill[src]
        bias = jnp.concatenate(
            [jnp.where(lane < fills % 256, 0.0, NEG), jnp.where(lane < fills // 256, 0.0, NEG)], 1
        )
        keys = recv[src, :, :HD]
        vals = jnp.concatenate([recv[src, :, HD:], ones], 1)
        for qb in range(WIDTH // blk):
            rows = pl.ds(qb * blk, blk)
            s = scores(rows, keys) + bias
            old = m[rows, :]
            new = jnp.maximum(old, jnp.max(s, 1, keepdims=True))
            alpha = jnp.exp2(old - new)
            p = jnp.exp2(s - jnp.concatenate([new, new], 1)).astype(BF16)
            part = jnp.dot(p, vals, preferred_element_type=F32)
            acc[rows, :] = acc[rows, :] * jnp.concatenate([alpha, alpha], 1) + part
            m[rows, :] = new

    def take_from(src):
        for d in (
            copy(send.at[src], recv.at[src], kv_s.at[0], kv_r.at[src], (src, t)),
            copy(sfill.at[src], rfill.at[src], f_s.at[0], f_r.at[src], (src, t)),
        ):
            d.wait_recv()
        attend(src)

    def take(i, k):
        dx, dy = hop(i // NC)
        take_from(at(x + NX - dx, y + NY - dy, i % NC))
        return k

    def run(lo, hi):
        lax.fori_loop(lo, hi, take, 0)

    attend(g)
    take_from(sib)
    total[...] = jnp.zeros_like(total)

    per_half = heads_n // 2

    def zcopy(hf, s, dst):
        z = (t + s) % NZ
        return copy(heads.at[hf, z], gath.at[g, hf, dst(z)], a_s.at[hf, s], a_r.at[hf, dst(z)], (g, z))

    def spread(hf):
        for s in range(1, NZ):
            zcopy(hf, s, lambda z: t).start()
        gath[g, hf, t] = heads[hf, t]

    def finalize():
        for hf in range(2):
            for h in range(per_half):
                rows = pl.ds((hf * per_half + h) * NEW, NEW)
                out = (acc[rows, :HD] / acc[rows, HD:]).astype(BF16)
                heads[hf, :, :, h * HD:(h + 1) * HD] = out.reshape(NZ, CHUNK, HD)
            if hf == 0:
                spread(0)

    def spread_in(hf):
        for s in range(1, NZ):
            zcopy(hf, s, lambda z: z).wait_recv()

    def piece(owner, lo, size):
        return gath.at[owner, lo // NZ, pl.ds(lo % NZ, size)]

    def arrived(owner, lo, size, quarter):
        part = piece(owner, lo, size)
        copy(part, part, g_s.at[0], g_r.at[owner, quarter], (sib, t)).wait_recv()

    def place(h, d1, d2, pc):
        return at(x + d1, y + d2, pc) if h == 0 else at(x + d2, y + d1, pc)

    PUSHES = {
        (0, 0): [((1, 0), 0, NZ, 0), ((3, 0), 0, NZ, 0), ((2, 0), 0, NZ, 0), ((0, 1), 0, NZ, 0), ((0, 3), 0, NZ, 0)],
        (3, 0): [((0, 1), 0, NZ, 0), ((0, 3), 0, NZ, 0)],
        (1, 0): [((0, 1), 0, NZ, 0), ((0, 3), 0, NZ, 0)],
        (2, 0): [((0, 1), 0, NZ, 0), ((0, 3), 0, NZ, 0)],
    }
    for d1 in range(4):
        PUSHES[(d1, 3)] = [((0, 1), 0, 4, 0)]
        PUSHES[(d1, 1)] = [((0, 3), 4, 4, 1)]
    first_sem, count = {}, 0
    for h in range(2):
        for d in ORDER:
            first_sem[(h, d)] = count
            count += len(PUSHES.get(d, ()))

    def pushes(h, d1, d2):
        owner = place(h, d1, d2, c)
        base = first_sem[(h, (d1, d2))]
        out = []
        for i, (to, lo, size, quarter) in enumerate(PUSHES.get((d1, d2), ())):
            part = piece(owner, NZ * h + lo, size)
            dev = place(h, to[0], to[1], c)
            out.append(copy(part, part, g_s.at[base + i], g_r.at[owner, 2 * h + quarter], (dev, t)))
        return out

    def share(h, d1, d2):
        owner = place(h, d1, d2, c)
        part = piece(owner, NZ * h, NZ)
        n = h * CHIPS + ORDER.index((d1, d2))
        return copy(part, part, b_s.at[n], b_r.at[owner, h], (sib, t))

    def event(h, d1, d2):
        owner = place(h, d1, d2, c)
        lo = NZ * h
        q = 2 * h
        last = d2 if d2 else d1
        if d2 == 2:
            arrived(owner, lo, 4, q)
            arrived(owner, lo + 4, 4, q + 1)
        elif last:
            arrived(owner, lo, NZ, q)
        for d in pushes(h, d1, d2):
            d.start()
        share(h, d1, d2).start()

    def shared_in(h, groups):
        for d2 in groups:
            for d1 in range(4):
                other = place(h, d1, d2, 1 - c)
                part = piece(other, NZ * h, NZ)
                copy(part, part, b_s.at[0], b_r.at[other, h], (sib, t)).wait_recv()

    def multiply(h, groups, *pcs):
        owners = [place(h, d1, d2, pc) for pc in pcs for d2 in groups for d1 in range(4)]
        rows = jnp.concatenate(
            [jnp.concatenate([gath[o, h, z] for o in owners], 0) for z in range(NZ)], 1
        )
        weights = wfull[:, h * half:(h + 1) * half].reshape(NZ * half, FEAT)
        got = jnp.dot(rows, weights, preferred_element_type=F32)
        for i, o in enumerate(owners):
            total[o] = total[o] + got[i * CHUNK:(i + 1) * CHUNK]

    def ocopy(s, e, pc, dst):
        z = (t + s) % NZ
        to = dst(z)
        here = z * 4 + e * 2 + pc if to is t else t * 4 + e * 2 + pc
        return copy(zout.at[here], obuf.at[e * 2 + pc, to], o_s.at[s, e, pc], o_r.at[to, e, pc], (g, z))

    def hand(pc, late):
        for s in range(1, NZ):
            z = (t + s) % NZ
            for e in range(2):
                if late is None:
                    ocopy(s, e, pc, lambda z: t).start()
                    continue
                far = ((z // 2 + NX - x) % NX == 2) | (((z % 2) * 2 + e + NY - y) % NY == 2)

                @pl.when(far if late else jnp.logical_not(far))
                def _():
                    ocopy(s, e, pc, lambda z: t).start()

    def finish(pc, late):
        for d1 in range(4):
            for d2 in range(4):
                if late is None or late == (d1 == 2 or d2 == 2):
                    o = at(x + d1, y + d2, pc)
                    zout[o] = total[o].astype(BF16)
        hand(pc, late)

    near = (0, 3, 1)
    every = (0, 3, 1, 2)

    def events(lo, hi):
        for d in ORDER[lo:hi]:
            for h in range(2):
                event(h, *d)

    def opening():
        finalize()
        spread(1)
        spread_in(0)
        event(0, 0, 0)
        spread_in(1)
        event(1, 0, 0)

    @pl.when(c == 0)
    def _():
        wpass(1)
        run(2, 12)
        wpass(2)
        run(12, 20)
        more()
        run(20, GRP)
        opening()
        events(1, 5)
        wpass(3)
        events(5, 16)
        wlast()
        for h in range(2):
            multiply(h, every, 0)
        finish(0, None)
        for h in range(2):
            shared_in(h, near)
            multiply(h, near, 1)
        finish(1, False)
        for h in range(2):
            shared_in(h, (2,))
            multiply(h, (2,), 1)

    @pl.when(c == 1)
    def _():
        wpass(1)
        wpass(2)
        more()
        run(2, 10)
        wpass(3)
        run(10, GRP)
        opening()
        events(1, 4)
        wlast()
        shared_in(0, every)
        multiply(0, every, 0)
        events(4, 8)
        shared_in(1, every)
        multiply(1, every, 0)
        events(8, 13)
        finish(0, None)
        multiply(0, near, 1)
        events(13, 14)
        multiply(1, near, 1)
        events(14, 16)
        finish(1, False)
        for h in range(2):
            multiply(h, (2,), 1)

    finish(1, True)
    obuf[:, t] = zout[pl.ds(t * 4, 4)]
    for s in range(1, NZ):
        for e in range(2):
            for pc in range(NC):
                ocopy(s, e, pc, lambda z: z).wait_recv()
    o_ref[...] = obuf[...]

    for d in kv_copies(sib, 0):
        d.wait_send()

    def sent(p, k, carry):
        for d in give_to(p, k):
            d.wait_send()
        return carry

    lax.fori_loop(EARLY + 1, CHIPS, functools.partial(sent, 0), 0)
    lax.fori_loop(1, CHIPS, functools.partial(sent, 1), 0)
    for s in range(1, NZ):
        for e in range(2):
            zcopy(e, s, lambda z: t).wait_send()
            for pc in range(NC):
                ocopy(s, e, pc, lambda z: t).wait_send()
    for n in range(NZ):
        wsend(n).wait_send()
    for h in range(2):
        for d in ORDER:
            share(h, *d).wait_send()
            for p in pushes(h, *d):
                p.wait_send()


def body(queries, span_kv, cache, block_owner, block_fill, out_weight):
    slots = cache.shape[0]
    any_ = pl.BlockSpec(memory_space=pl.ANY)
    vmem = pl.BlockSpec(memory_space=pltpu.VMEM)
    dma = pltpu.SemaphoreType.DMA
    out = pl.pallas_call(
        main_kernel,
        out_shape=jax.ShapeDtypeStruct((GRP // NZ, NZ, CHUNK, FEAT), BF16),
        in_specs=[any_] * 6,
        out_specs=vmem,
        scratch_shapes=[
            pltpu.VMEM((1, slots), jnp.int32),
            pltpu.VMEM((1, slots), jnp.int32),
            pltpu.VMEM((NEW, WIDTH), BF16),
            pltpu.VMEM((NEW, 2 * HD), BF16),
            pltpu.VMEM((slots, KB, 2 * HD), BF16),
            pltpu.VMEM((GRP, KB), jnp.int32),
            pltpu.SMEM((GRP, KB), jnp.int32),
            pltpu.VMEM((GRP, CAP * KB, 2 * HD), BF16),
            pltpu.VMEM((GRP, 1, KB), jnp.int32),
            pltpu.VMEM((GRP, CAP * KB, 2 * HD), BF16),
            pltpu.VMEM((GRP, 1, KB), jnp.int32),
            pltpu.VMEM((WIDTH, HD), BF16),
            pltpu.VMEM((WIDTH, HD), F32),
            pltpu.VMEM((WIDTH, 2 * HD), F32),
            pltpu.VMEM((NZ, WIDTH, FEAT), BF16),
            pltpu.VMEM((2, NZ, CHUNK, WIDTH // 2), BF16),
            pltpu.VMEM((GRP, 2, NZ, CHUNK, WIDTH // 2), BF16),
            pltpu.VMEM((GRP, CHUNK, FEAT), F32),
            pltpu.VMEM((GRP, CHUNK, FEAT), BF16),
            pltpu.VMEM((GRP // NZ, NZ, CHUNK, FEAT), BF16),
            dma((7,)),
            dma((GRP,)), dma((GRP,)), dma((GRP,)), dma((GRP,)),
            dma((NZ,)), dma((NZ, 2)),
            dma((2, NZ)), dma((2, NZ)),
            dma((40,)), dma((GRP, 4)),
            dma((32,)), dma((GRP, 2)),
            dma((NZ, 2, NC)), dma((NZ, 2, NC)),
        ],
        compiler_params=pltpu.CompilerParams(
            collective_id=0, has_side_effects=True, vmem_limit_bytes=VMEM_LIMIT
        ),
    )(
        block_owner.reshape(1, slots),
        block_fill.reshape(1, slots),
        queries.reshape(NEW, WIDTH),
        span_kv.reshape(NEW, 2 * HD),
        cache.reshape(slots, KB, 2 * HD),
        out_weight,
    )
    return out.reshape(GRP // NZ * NEW, FEAT)


def solution(mesh):
    in_specs = (
        P("grp", None, "tp"),
        P("grp", None, "tp", None),
        P("grp", None, "tp", None),
        P("grp", None),
        P("grp", None),
        P("tp", "grp"),
    )
    out_specs = P("tp", "grp")
    return jax.shard_map(body, mesh=mesh, in_specs=in_specs, out_specs=out_specs, check_vma=False)
```

```python
import functools

import jax
import jax.numpy as jnp
from jax import lax
from jax.experimental import pallas as pl
from jax.experimental.pallas import tpu as pltpu
from jax.sharding import PartitionSpec as P

MESH = pl.DeviceIdType.MESH
NX, NY, NC, NZ = 4, 4, 2, 8
CHIPS = NX * NY
GRP = CHIPS * NC
CAP = 2
KB = 128
HD = 128
NEW = 128
WIDTH = 1024
FEAT = 256
CHUNK = NEW // NZ
NEG = -1e30
EARLY = 12
SWITCH = 20
VMEM_LIMIT = 62 * 1024 * 1024
LOG2E = 1.4426950408889634
F32 = jnp.float32
BF16 = jnp.bfloat16
ORDER = ((0, 0), (3, 0), (1, 0), (0, 3), (0, 1), (2, 0), (3, 3), (3, 1), (1, 3), (1, 1), (0, 2), (2, 3), (2, 1), (3, 2), (1, 2), (2, 2))


def main_kernel(
    owner_hbm, fill_hbm, q_hbm, span_hbm, cache_hbm, w_hbm, o_ref,
    owner_ref, fill_ref, q_ref, span_ref, cache_ref, table_v, table,
    send, sfill, recv, rfill, qs, m, acc, wfull, heads, gath, total, zout, obuf,
    in_s, kv_s, kv_r, f_s, f_r, w_s, w_r, a_s, a_r, g_s, g_r, b_s, b_r, o_s, o_r,
):
    g = lax.axis_index("grp")
    t = lax.axis_index("tp")
    x, y, c = g // (NY * NC), (g // NC) % NY, g % NC

    def at(px, py, pc):
        return (px % NX) * (NY * NC) + (py % NY) * NC + pc

    sib = at(x, y, 1 - c)

    def copy(src, dst, ssem, rsem, dev):
        return pltpu.make_async_remote_copy(
            src_ref=src, dst_ref=dst, send_sem=ssem, recv_sem=rsem, device_id=dev, device_id_type=MESH
        )

    barrier = pltpu.get_barrier_semaphore()

    def greet(s, k):
        pl.semaphore_signal(barrier, inc=1, device_id=((g + s) % GRP, t), device_id_type=MESH)
        return k

    lax.fori_loop(1, GRP, greet, 0)
    for s in range(1, NZ):
        pl.semaphore_signal(barrier, inc=1, device_id=(g, (t + s) % NZ), device_id_type=MESH)
    loads = [
        pltpu.make_async_copy(owner_hbm, owner_ref, in_s.at[0]),
        pltpu.make_async_copy(fill_hbm, fill_ref, in_s.at[1]),
        pltpu.make_async_copy(cache_hbm, cache_ref, in_s.at[2]),
        pltpu.make_async_copy(w_hbm, wfull.at[t], in_s.at[3]),
        pltpu.make_async_copy(q_hbm, q_ref, in_s.at[4]),
        pltpu.make_async_copy(span_hbm, span_ref, in_s.at[5]),
    ]
    for d in loads:
        d.start()

    loads[0].wait()
    loads[1].wait()
    slots = owner_ref.shape[1]
    shape = (GRP, slots)
    own = jnp.broadcast_to(owner_ref[...], shape)
    fill = jnp.broadcast_to(fill_ref[...], shape)
    block = lax.broadcasted_iota(jnp.int32, shape, 1)
    hit = own == lax.broadcasted_iota(jnp.int32, shape, 0)
    low = jnp.min(jnp.where(hit, block, slots), 1, keepdims=True)
    high = jnp.max(jnp.where(hit, block, -1), 1, keepdims=True)
    code = jnp.sum(jnp.where(hit, jnp.where(block == low, fill, fill * 256), 0), 1, keepdims=True)
    lane = lax.broadcasted_iota(jnp.int32, (GRP, KB), 1)
    table_v[...] = jnp.where(lane == 0, jnp.minimum(low, slots - 1), jnp.maximum(high, 0))
    sfill[...] = jnp.broadcast_to(code, (GRP, KB)).reshape(GRP, 1, KB)
    to_smem = pltpu.make_async_copy(table_v, table, in_s.at[6])
    to_smem.start()
    to_smem.wait()
    loads[2].wait()

    def load(dst):
        return cache_ref[table[dst, 0]], cache_ref[table[dst, 1]]

    def pack(s, k):
        dst = (g + s) % GRP
        first, second = load(dst)
        send[dst, :KB] = first
        send[dst, KB:] = second
        return k

    lax.fori_loop(1, GRP, pack, 0)
    first, second = load(g)
    recv[g, :KB] = first
    recv[g, KB:] = second
    rfill[g] = sfill[g]
    loads[3].wait()
    pl.semaphore_wait(barrier, GRP - 1 + NZ - 1)

    up, down = (t + 1) % NZ, (t + NZ - 1) % NZ
    half = WIDTH // 2

    def wcopy(n, z, lo, size, k, dev):
        part = wfull.at[z, pl.ds(lo, size)]
        return copy(part, part, w_s.at[n], w_r.at[z, k], (g, dev))

    WSENDS = [
        (0, 0, 0, WIDTH, 0, 1), (1, 0, 0, WIDTH, 0, -1), (2, -1, 0, WIDTH, 0, 1), (3, 1, 0, WIDTH, 0, -1),
        (4, -2, 0, WIDTH, 0, 1), (5, 2, 0, WIDTH, 0, -1), (6, -3, 0, half, 0, 1), (7, 3, half, half, 1, -1),
    ]

    def wsend(n):
        n, dz, lo, size, k, way = WSENDS[n]
        return wcopy(n, (t + NZ + dz) % NZ, lo, size, k, up if way == 1 else down)

    wsend(0).start()
    wsend(1).start()

    def wpass(j):
        wcopy(0, (t + NZ - j) % NZ, 0, WIDTH, 0, up).wait_recv()
        wsend(2 * j).start()
        wcopy(0, (t + j) % NZ, 0, WIDTH, 0, down).wait_recv()
        wsend(2 * j + 1).start()

    def wlast():
        opposite = (t + 4) % NZ
        wcopy(0, opposite, 0, half, 0, up).wait_recv()
        wcopy(0, opposite, half, half, 1, down).wait_recv()

    def hop(k):
        o = (k * 5) % CHIPS
        return o // NY, o % NY

    def kv_copies(dst, n):
        return (
            copy(send.at[dst], recv.at[g], kv_s.at[n], kv_r.at[g], (dst, t)),
            copy(sfill.at[dst], rfill.at[g], f_s.at[n], f_r.at[g], (dst, t)),
        )

    def give_to(p, k):
        dx, dy = hop(k)
        return kv_copies(at(x + dx, y + dy, p), p * CHIPS + k)

    def give(p, k, carry):
        for d in give_to(p, k):
            d.start()
        return carry

    for d in kv_copies(sib, 0):
        d.start()
    lax.fori_loop(1, CHIPS, functools.partial(give, 0), 0)

    def more():
        def done(k, carry):
            for d in give_to(0, k):
                d.wait_send()
            return carry

        lax.fori_loop(1, EARLY + 1, done, 0)
        lax.fori_loop(1, CHIPS, functools.partial(give, 1), 0)

    loads[4].wait()
    loads[5].wait()

    heads_n = WIDTH // HD
    for h in range(heads_n):
        qs[h * NEW:(h + 1) * NEW, :] = q_ref[:, h * HD:(h + 1) * HD]
    factor = LOG2E / HD**0.5
    blk = 256
    ones = jnp.ones((CAP * KB, HD), BF16)

    def scores(rows, keys):
        return lax.dot_general(qs[rows, :], keys, (((1,), (1,)), ((), ())), preferred_element_type=F32) * factor

    span_k, span_v = span_ref[:, :HD], span_ref[:, HD:]
    span_aug = jnp.concatenate([span_v, ones[:NEW]], 1)
    row = lax.broadcasted_iota(jnp.int32, (blk, NEW), 0) % NEW
    col = lax.broadcasted_iota(jnp.int32, (blk, NEW), 1)
    for qb in range(WIDTH // blk):
        rows = pl.ds(qb * blk, blk)
        s = jnp.where(col <= row, scores(rows, span_k), NEG)
        top = jnp.max(s, 1, keepdims=True)
        m[rows, :] = jnp.broadcast_to(top, (blk, HD))
        p = jnp.exp2(s - top).astype(BF16)
        acc[rows, :] = jnp.dot(p, span_aug, preferred_element_type=F32)

    lane = lax.broadcasted_iota(jnp.int32, (1, KB), 1)

    def attend(src):
        fills = rfill[src]
        bias = jnp.concatenate(
            [jnp.where(lane < fills % 256, 0.0, NEG), jnp.where(lane < fills // 256, 0.0, NEG)], 1
        )
        keys = recv[src, :, :HD]
        vals = jnp.concatenate([recv[src, :, HD:], ones], 1)
        for qb in range(WIDTH // blk):
            rows = pl.ds(qb * blk, blk)
            s = scores(rows, keys) + bias
            old = m[rows, :]
            new = jnp.maximum(old, jnp.max(s, 1, keepdims=True))
            alpha = jnp.exp2(old - new)
            p = jnp.exp2(s - jnp.concatenate([new, new], 1)).astype(BF16)
            part = jnp.dot(p, vals, preferred_element_type=F32)
            acc[rows, :] = acc[rows, :] * jnp.concatenate([alpha, alpha], 1) + part
            m[rows, :] = new

    def take_from(src):
        for d in (
            copy(send.at[src], recv.at[src], kv_s.at[0], kv_r.at[src], (src, t)),
            copy(sfill.at[src], rfill.at[src], f_s.at[0], f_r.at[src], (src, t)),
        ):
            d.wait_recv()
        attend(src)

    def take(i, k):
        dx, dy = hop(i // NC)
        take_from(at(x + NX - dx, y + NY - dy, i % NC))
        return k

    def run(lo, hi):
        lax.fori_loop(lo, hi, take, 0)

    attend(g)
    take_from(sib)
    total[...] = jnp.zeros_like(total)

    per_half = heads_n // 2

    def zcopy(hf, s, dst):
        z = (t + s) % NZ
        return copy(heads.at[hf, z], gath.at[g, hf, dst(z)], a_s.at[hf, s], a_r.at[hf, dst(z)], (g, z))

    def spread(hf):
        for s in range(1, NZ):
            zcopy(hf, s, lambda z: t).start()
        gath[g, hf, t] = heads[hf, t]

    def finalize():
        for hf in range(2):
            for h in range(per_half):
                rows = pl.ds((hf * per_half + h) * NEW, NEW)
                out = (acc[rows, :HD] / acc[rows, HD:]).astype(BF16)
                heads[hf, :, :, h * HD:(h + 1) * HD] = out.reshape(NZ, CHUNK, HD)
            if hf == 0:
                spread(0)

    def spread_in(hf):
        for s in range(1, NZ):
            zcopy(hf, s, lambda z: z).wait_recv()

    def piece(owner, lo, size):
        return gath.at[owner, lo // NZ, pl.ds(lo % NZ, size)]

    def arrived(owner, lo, size, quarter):
        part = piece(owner, lo, size)
        copy(part, part, g_s.at[0], g_r.at[owner, quarter], (sib, t)).wait_recv()

    def place(h, d1, d2, pc):
        return at(x + d1, y + d2, pc) if h == 0 else at(x + d2, y + d1, pc)

    PUSHES = {
        (0, 0): [((1, 0), 0, NZ, 0), ((3, 0), 0, NZ, 0), ((2, 0), 0, NZ, 0), ((0, 1), 0, NZ, 0), ((0, 3), 0, NZ, 0)],
        (3, 0): [((0, 1), 0, NZ, 0), ((0, 3), 0, NZ, 0)],
        (1, 0): [((0, 1), 0, NZ, 0), ((0, 3), 0, NZ, 0)],
        (2, 0): [((0, 1), 0, NZ, 0), ((0, 3), 0, NZ, 0)],
    }
    for d1 in range(4):
        PUSHES[(d1, 3)] = [((0, 1), 0, 4, 0)]
        PUSHES[(d1, 1)] = [((0, 3), 4, 4, 1)]
    first_sem, count = {}, 0
    for h in range(2):
        for d in ORDER:
            first_sem[(h, d)] = count
            count += len(PUSHES.get(d, ()))

    def pushes(h, d1, d2):
        owner = place(h, d1, d2, c)
        base = first_sem[(h, (d1, d2))]
        out = []
        for i, (to, lo, size, quarter) in enumerate(PUSHES.get((d1, d2), ())):
            part = piece(owner, NZ * h + lo, size)
            dev = place(h, to[0], to[1], c)
            out.append(copy(part, part, g_s.at[base + i], g_r.at[owner, 2 * h + quarter], (dev, t)))
        return out

    def share(h, d1, d2):
        owner = place(h, d1, d2, c)
        part = piece(owner, NZ * h, NZ)
        n = h * CHIPS + ORDER.index((d1, d2))
        return copy(part, part, b_s.at[n], b_r.at[owner, h], (sib, t))

    def event(h, d1, d2):
        owner = place(h, d1, d2, c)
        lo = NZ * h
        q = 2 * h
        last = d2 if d2 else d1
        if d2 == 2:
            arrived(owner, lo, 4, q)
            arrived(owner, lo + 4, 4, q + 1)
        elif last:
            arrived(owner, lo, NZ, q)
        for d in pushes(h, d1, d2):
            d.start()
        share(h, d1, d2).start()

    def shared_in(h, groups):
        for d2 in groups:
            for d1 in range(4):
                other = place(h, d1, d2, 1 - c)
                part = piece(other, NZ * h, NZ)
                copy(part, part, b_s.at[0], b_r.at[other, h], (sib, t)).wait_recv()

    def multiply(h, groups, *pcs):
        owners = [place(h, d1, d2, pc) for pc in pcs for d2 in groups for d1 in range(4)]
        rows = jnp.concatenate(
            [jnp.concatenate([gath[o, h, z] for o in owners], 0) for z in range(NZ)], 1
        )
        weights = wfull[:, h * half:(h + 1) * half].reshape(NZ * half, FEAT)
        got = jnp.dot(rows, weights, preferred_element_type=F32)
        for i, o in enumerate(owners):
            total[o] = total[o] + got[i * CHUNK:(i + 1) * CHUNK]

    def ocopy(s, e, pc, dst):
        z = (t + s) % NZ
        to = dst(z)
        here = z * 4 + e * 2 + pc if to is t else t * 4 + e * 2 + pc
        return copy(zout.at[here], obuf.at[e * 2 + pc, to], o_s.at[s, e, pc], o_r.at[to, e, pc], (g, z))

    def hand(pc, late):
        for s in range(1, NZ):
            z = (t + s) % NZ
            for e in range(2):
                if late is None:
                    ocopy(s, e, pc, lambda z: t).start()
                    continue
                far = ((z // 2 + NX - x) % NX == 2) | (((z % 2) * 2 + e + NY - y) % NY == 2)

                @pl.when(far if late else jnp.logical_not(far))
                def _():
                    ocopy(s, e, pc, lambda z: t).start()

    def finish(pc, late):
        for d1 in range(4):
            for d2 in range(4):
                if late is None or late == (d1 == 2 or d2 == 2):
                    o = at(x + d1, y + d2, pc)
                    zout[o] = total[o].astype(BF16)
        hand(pc, late)

    near = (0, 3, 1)
    every = (0, 3, 1, 2)

    def events(lo, hi):
        for d in ORDER[lo:hi]:
            for h in range(2):
                event(h, *d)

    def opening():
        finalize()
        spread(1)
        spread_in(0)
        event(0, 0, 0)
        spread_in(1)
        event(1, 0, 0)

    @pl.when(c == 0)
    def _():
        wpass(1)
        run(2, 12)
        wpass(2)
        run(12, 20)
        more()
        run(20, GRP)
        opening()
        events(1, 5)
        wpass(3)
        events(5, 16)
        wlast()
        for h in range(2):
            multiply(h, every, 0)
        finish(0, None)
        for h in range(2):
            shared_in(h, near)
            multiply(h, near, 1)
        finish(1, False)
        for h in range(2):
            shared_in(h, (2,))
            multiply(h, (2,), 1)

    @pl.when(c == 1)
    def _():
        wpass(1)
        wpass(2)
        more()
        run(2, 10)
        wpass(3)
        run(10, GRP)
        opening()
        events(1, 4)
        wlast()
        shared_in(0, every)
        multiply(0, every, 0)
        events(4, 8)
        shared_in(1, every)
        multiply(1, every, 0)
        events(8, 13)
        finish(0, None)
        multiply(0, near, 1)
        events(13, 14)
        multiply(1, near, 1)
        events(14, 15)
        finish(1, False)
        for h in range(2):
            event(h, *ORDER[15])
            multiply(h, (2,), 1)

    finish(1, True)
    obuf[:, t] = zout[pl.ds(t * 4, 4)]
    for s in range(1, NZ):
        for e in range(2):
            for pc in range(NC):
                ocopy(s, e, pc, lambda z: z).wait_recv()
    o_ref[...] = obuf[...]

    for d in kv_copies(sib, 0):
        d.wait_send()

    def sent(p, k, carry):
        for d in give_to(p, k):
            d.wait_send()
        return carry

    lax.fori_loop(EARLY + 1, CHIPS, functools.partial(sent, 0), 0)
    lax.fori_loop(1, CHIPS, functools.partial(sent, 1), 0)
    for s in range(1, NZ):
        for e in range(2):
            zcopy(e, s, lambda z: t).wait_send()
            for pc in range(NC):
                ocopy(s, e, pc, lambda z: t).wait_send()
    for n in range(NZ):
        wsend(n).wait_send()
    for h in range(2):
        for d in ORDER:
            share(h, *d).wait_send()
            for p in pushes(h, *d):
                p.wait_send()


def body(queries, span_kv, cache, block_owner, block_fill, out_weight):
    slots = cache.shape[0]
    any_ = pl.BlockSpec(memory_space=pl.ANY)
    vmem = pl.BlockSpec(memory_space=pltpu.VMEM)
    dma = pltpu.SemaphoreType.DMA
    out = pl.pallas_call(
        main_kernel,
        out_shape=jax.ShapeDtypeStruct((GRP // NZ, NZ, CHUNK, FEAT), BF16),
        in_specs=[any_] * 6,
        out_specs=vmem,
        scratch_shapes=[
            pltpu.VMEM((1, slots), jnp.int32),
            pltpu.VMEM((1, slots), jnp.int32),
            pltpu.VMEM((NEW, WIDTH), BF16),
            pltpu.VMEM((NEW, 2 * HD), BF16),
            pltpu.VMEM((slots, KB, 2 * HD), BF16),
            pltpu.VMEM((GRP, KB), jnp.int32),
            pltpu.SMEM((GRP, KB), jnp.int32),
            pltpu.VMEM((GRP, CAP * KB, 2 * HD), BF16),
            pltpu.VMEM((GRP, 1, KB), jnp.int32),
            pltpu.VMEM((GRP, CAP * KB, 2 * HD), BF16),
            pltpu.VMEM((GRP, 1, KB), jnp.int32),
            pltpu.VMEM((WIDTH, HD), BF16),
            pltpu.VMEM((WIDTH, HD), F32),
            pltpu.VMEM((WIDTH, 2 * HD), F32),
            pltpu.VMEM((NZ, WIDTH, FEAT), BF16),
            pltpu.VMEM((2, NZ, CHUNK, WIDTH // 2), BF16),
            pltpu.VMEM((GRP, 2, NZ, CHUNK, WIDTH // 2), BF16),
            pltpu.VMEM((GRP, CHUNK, FEAT), F32),
            pltpu.VMEM((GRP, CHUNK, FEAT), BF16),
            pltpu.VMEM((GRP // NZ, NZ, CHUNK, FEAT), BF16),
            dma((7,)),
            dma((GRP,)), dma((GRP,)), dma((GRP,)), dma((GRP,)),
            dma((NZ,)), dma((NZ, 2)),
            dma((2, NZ)), dma((2, NZ)),
            dma((40,)), dma((GRP, 4)),
            dma((32,)), dma((GRP, 2)),
            dma((NZ, 2, NC)), dma((NZ, 2, NC)),
        ],
        compiler_params=pltpu.CompilerParams(
            collective_id=0, has_side_effects=True, vmem_limit_bytes=VMEM_LIMIT
        ),
    )(
        block_owner.reshape(1, slots),
        block_fill.reshape(1, slots),
        queries.reshape(NEW, WIDTH),
        span_kv.reshape(NEW, 2 * HD),
        cache.reshape(slots, KB, 2 * HD),
        out_weight,
    )
    return out.reshape(GRP // NZ * NEW, FEAT)


def solution(mesh):
    in_specs = (
        P("grp", None, "tp"),
        P("grp", None, "tp", None),
        P("grp", None, "tp", None),
        P("grp", None),
        P("grp", None),
        P("tp", "grp"),
    )
    out_specs = P("tp", "grp")
    return jax.shard_map(body, mesh=mesh, in_specs=in_specs, out_specs=out_specs, check_vma=False)
```
